256 devices in a mesh: section: 2 (over x_lo), dp: 4 (over y), mp: 32 (over z, x_hi, core).
Axes of the slice: x: 4 (x_hi: 2, x_lo: 2; x = x_hi * 2 + x_lo), y: 4, z: 8, core: 2. Of those that a mesh axis runs over, the one named last changes fastest.
Arguments:
- tokens: bfloat16 [4, 128, 8192], P('dp', None, 'mp'), may hold values from -6 to 6
- par_gain: float32 [2, 8192], P('section'), may hold values from 0.5 to 1.5
- par_wq: bfloat16 [2, 8192, 8192], P('section', 'dp', 'mp'), may hold values from -1 to 1
- par_wk: bfloat16 [2, 8192, 1024], P('section', 'dp', 'mp'), may hold values from -1 to 1
- par_wv: bfloat16 [2, 8192, 1024], P('section', 'dp', 'mp'), may hold values from -0.0625 to 0.0625
- par_wo: bfloat16 [2, 8192, 8192], P('section', 'mp', 'dp'), may hold values from -0.0625 to 0.0625
- var_wq: bfloat16 [2, 8192, 8192], P('section', 'dp', 'mp'), may hold values from -1 to 1
- var_wk: bfloat16 [2, 8192, 1024], P('section', 'dp', 'mp'), may hold values from -1 to 1
- var_wv: bfloat16 [2, 8192, 1024], P('section', 'dp', 'mp'), may hold values from -0.0625 to 0.0625
- var_wo: bfloat16 [2, 8192, 8192], P('section', 'mp', 'dp'), may hold values from -0.0625 to 0.0625
- lin_w: bfloat16 [2, 8192, 8192], P('section', 'dp', 'mp'), may hold values from -0.0625 to 0.0625
- windows: int32 [2], P('section'), may hold values from 32 to 64
Outputs:
- layer_out: bfloat16 [2, 4, 128, 8192], P('section', 'dp', None, 'mp')
- grad_wq: float32 [2, 8192, 8192], P('section', 'dp', 'mp')
- grad_wk: float32 [2, 8192, 1024], P('section', 'dp', 'mp')
- grad_wv: float32 [2, 8192, 1024], P('section', 'dp', 'mp')
- grad_wo: float32 [2, 8192, 8192], P('section', 'mp', 'dp')
- grad_lin: float32 [2, 8192, 8192], P('section', 'dp', 'mp')
The draws below stay inside these ranges and needn't reach their ends.
Inputs may be any that keep to these rules, and one draw needn't show every extreme that they name: `windows`: window length of each layer's windowed variant.
All inputs are finite; a program needn't handle non-finite values.
Results may differ from the reference program's by a relative error of at most 0.025.
Values may be sent and summed in bfloat16 or wider, within the bound.
No kernel may reach another device: no remote copies, remote signals or barrier semaphores. Data moves between devices by JAX's collectives and lax.ppermute only.
A program may use at most 192 MiB of HBM per device.

```python
import jax
import jax.numpy as jnp
from jax import lax

D = 8192
HQ = 64
KVH = 8
HD = 128
SEQ = 128
MB_DEV = 1
LAYERS = 2
MICRO = 4
TOKENS = 512


def drawn_weight(key, columns):
    values = jax.random.normal(key, (LAYERS, D, columns), jnp.float32)
    return jnp.clip(values, -6.0, 6.0) * D ** (-0.5)


def draw_tokens(key, part):
    key = jax.random.fold_in(key, 7)
    values = jnp.clip(jax.random.normal(key, (MICRO, SEQ, D), jnp.float32), -6.0, 6.0)
    return values.astype(jnp.bfloat16)


def draw_par_wq(key, part):
    key = jax.random.fold_in(key, 11)
    values = drawn_weight(key, HQ * HD)
    return values.astype(jnp.bfloat16)


def draw_par_wk(key, part):
    key = jax.random.fold_in(key, 13)
    values = drawn_weight(key, KVH * HD)
    return values.astype(jnp.bfloat16)


def draw_var_wq(key, part):
    key = jax.random.fold_in(key, 17)
    values = drawn_weight(key, HQ * HD)
    return values.astype(jnp.bfloat16)


def draw_var_wk(key, part):
    key = jax.random.fold_in(key, 19)
    values = drawn_weight(key, KVH * HD)
    return values.astype(jnp.bfloat16)


def block_levels(stream_key, dims, cuts, low, largest):
    level, own = 1.0, jax.random.fold_in(stream_key, 6)
    for axis_at, shards_of in cuts:
        draws = jnp.exp(jax.random.uniform(jax.random.fold_in(own, axis_at), (shards_of,), jnp.float32, low / len(cuts), largest / len(cuts)))
        level = level * jnp.repeat(draws, dims[axis_at] // shards_of).reshape([-1 if axis == axis_at else 1 for axis in range(len(dims))])
    return level


def noise(stream_key, dims, deviation, reach, cuts=(), kind=jnp.bfloat16):
    loudness = block_levels(stream_key, dims, cuts, -0.22, 0.18) if cuts else 1.0
    result = jax.random.normal(stream_key, dims, jnp.float32) * deviation * loudness
    return jnp.minimum(jnp.maximum(result, -reach), reach).astype(kind)


def setup_inputs(seed: int = 0) -> dict:
    seeds = jax.random.split(jax.random.key(seed), 13)
    return {
        "tokens": draw_tokens(jax.random.fold_in(seeds[12], 71), 0),
        "par_gain": jnp.clip(1.0 + 0.1 * jax.random.normal(seeds[1], (LAYERS, D), jnp.float32), 0.5, 1.5),
        "par_wq": draw_par_wq(jax.random.fold_in(seeds[12], 71), 0),
        "par_wk": draw_par_wk(jax.random.fold_in(seeds[12], 71), 0),
        "par_wv": noise(seeds[4], (LAYERS, D, KVH * HD), D ** -0.5, 0.0625, ((0, 2), (1, 4), (2, 32))),
        "par_wo": noise(seeds[5], (LAYERS, HQ * HD, D), (HQ * HD) ** -0.5, 0.0625, ((0, 2), (1, 32), (2, 4))),
        "var_wq": draw_var_wq(jax.random.fold_in(seeds[12], 71), 0),
        "var_wk": draw_var_wk(jax.random.fold_in(seeds[12], 71), 0),
        "var_wv": noise(seeds[8], (LAYERS, D, KVH * HD), D ** -0.5, 0.0625, ((0, 2), (1, 4), (2, 32))),
        "var_wo": noise(seeds[9], (LAYERS, HQ * HD, D), (HQ * HD) ** -0.5, 0.0625, ((0, 2), (1, 32), (2, 4))),
        "lin_w": noise(seeds[10], (LAYERS, D, D), D ** -0.5, 0.0625, ((0, 2), (1, 4), (2, 32))),
        "windows": jax.random.randint(seeds[11], (LAYERS,), SEQ // 4, SEQ // 2 + 1).astype(jnp.int32),
    }


def bround(values):
    return lax.optimization_barrier(values.astype(jnp.bfloat16))

def tdot(left, right):
    return lax.dot_general(left, right, (((0,), (0,)), ((), ())), preferred_element_type=jnp.float32)

def norm_rows(hidden, gain_row):
    values = hidden.astype(jnp.float32)
    scaled = values * lax.rsqrt(lax.optimization_barrier(jnp.mean(values * values, axis=-1, keepdims=True)) + 1e-05)
    return bround(scaled * gain_row)

def forward_heads(normed, weight_q, weight_k, weight_v, keep_mask):
    length = normed.shape[0]
    queries = bround(jnp.dot(normed, weight_q, preferred_element_type=jnp.float32)).reshape(length, KVH, HQ // KVH, HD)
    key_heads = bround(jnp.dot(normed, weight_k, preferred_element_type=jnp.float32)).reshape(length, KVH, HD)
    value_heads = bround(jnp.dot(normed, weight_v, preferred_element_type=jnp.float32)).reshape(length, KVH, HD)
    scores = jnp.einsum('ikgd,jkd->kgij', queries.astype(jnp.float32), key_heads.astype(jnp.float32)) * HD ** (-0.5)
    scores = jnp.where(keep_mask, scores, -1e+30)
    probs = jax.nn.softmax(scores, axis=-1)
    probs_b = bround(probs)
    context = jnp.einsum('kgij,jkd->ikgd', probs_b.astype(jnp.float32), value_heads.astype(jnp.float32))
    context = bround(context).reshape(length, HQ * HD)
    return (queries, key_heads, value_heads, probs, probs_b, context)

def backward_heads(queries, key_heads, value_heads, probs, probs_b, grad_context):
    length = grad_context.shape[0]
    grad_four = grad_context.reshape(length, KVH, HQ // KVH, HD).astype(jnp.float32)
    grad_probs = jnp.einsum('ikgd,jkd->kgij', grad_four, value_heads.astype(jnp.float32))
    grad_scores = probs * (grad_probs - lax.optimization_barrier(jnp.sum(grad_probs * probs, axis=-1, keepdims=True)))
    grad_scaled = bround(grad_scores * HD ** (-0.5)).astype(jnp.float32)
    grad_q = bround(jnp.einsum('kgij,jkd->ikgd', grad_scaled, key_heads.astype(jnp.float32))).reshape(length, HQ * HD)
    grad_k = bround(jnp.einsum('kgij,ikgd->jkd', grad_scaled, queries.astype(jnp.float32))).reshape(length, KVH * HD)
    grad_v = bround(jnp.einsum('kgij,ikgd->jkd', probs_b.astype(jnp.float32), grad_four)).reshape(length, KVH * HD)
    return (grad_q, grad_k, grad_v)

def reference(tokens, par_gain, par_wq, par_wk, par_wv, par_wo, var_wq, var_wk, var_wv, var_wo, lin_w, windows):
    inv_scale = float(TOKENS) ** (-0.5)
    positions = jnp.arange(SEQ, dtype=jnp.int32)
    causal = positions[None, :] <= positions[:, None]
    hidden = tokens
    layer_list = []
    grad_lists = [[], [], [], [], []]
    for layer in range(LAYERS):
        windowed = causal & (positions[None, :] > positions[:, None] - windows[layer])
        shapes = [(D, HQ * HD), (D, KVH * HD), (D, KVH * HD), (HQ * HD, D), (D, D)]
        totals = [jnp.zeros(shape, jnp.float32) for shape in shapes]
        partial_value = [jnp.zeros(shape, jnp.float32) for shape in shapes]
        produced = []
        for micro_index in range(MICRO):
            current = hidden[micro_index]
            normed = norm_rows(current, par_gain[layer])
            parent_heads = forward_heads(normed, par_wq[layer], par_wk[layer], par_wv[layer], causal)
            target = jnp.dot(parent_heads[5], par_wo[layer], preferred_element_type=jnp.float32)
            produced.append((current.astype(jnp.float32) + target).astype(jnp.bfloat16))
            student_heads = forward_heads(normed, var_wq[layer], var_wk[layer], var_wv[layer], windowed)
            student = jnp.dot(student_heads[5], var_wo[layer], preferred_element_type=jnp.float32)
            linear = jnp.dot(normed, lin_w[layer], preferred_element_type=jnp.float32)
            grad_student = bround((student - target) * inv_scale)
            grad_linear = bround((linear - target) * inv_scale)
            grad_context = bround(jnp.dot(grad_student, var_wo[layer].T, preferred_element_type=jnp.float32))
            grad_q, grad_k, grad_v = backward_heads(*student_heads[:5], grad_context)
            terms = (tdot(normed, grad_q), tdot(normed, grad_k), tdot(normed, grad_v), tdot(student_heads[5], grad_student), tdot(normed, grad_linear))
            partial_value = [old + new for old, new in zip(partial_value, terms)]
            if (micro_index + 1) % MB_DEV == 0:
                totals = [old + bround(part).astype(jnp.float32) for old, part in zip(totals, partial_value)]
                partial_value = [jnp.zeros(shape, jnp.float32) for shape in shapes]
        hidden = jnp.stack(produced)
        layer_list.append(hidden)
        for index in range(5):
            grad_lists[index].append(totals[index])
    return (jnp.stack(layer_list), jnp.stack(grad_lists[0]), jnp.stack(grad_lists[1]), jnp.stack(grad_lists[2]), jnp.stack(grad_lists[3]), jnp.stack(grad_lists[4]))
```

```python
import functools

import jax
import jax.numpy as jnp
from jax import lax
from jax.experimental import pallas as pl
from jax.experimental.pallas import tpu as pltpu
from jax.sharding import Mesh, PartitionSpec as P

HQ = 64
KVH = 8
HD = 128
MP = ("zh", "zl", "xh", "core")
Z = ("zh", "zl")
BF = jnp.bfloat16
F32 = jnp.float32


def dot(left, right, dims):
    return lax.dot_general(left, right, (dims, ((), ())), preferred_element_type=F32)


def shift_table(count, distance):
    return [(i, (i + distance) % count) for i in range(count)]


def ordered(own, other, at):
    return jnp.where(at == 0, jnp.stack([own, other]), jnp.stack([other, own]))


def partner(block, axis):
    return lax.ppermute(block, axis, [(0, 1), (1, 0)])


def turn_table(flip):
    return [
        ((a * 4 + b) * 2 + h, (b * 4 + a) * 2 + (h ^ flip))
        for a in range(4)
        for b in range(4)
        for h in range(2)
    ]


def turned(block, flip=0):
    return lax.ppermute(block, ("dp", "zh", "xh"), turn_table(flip))


def put(buffer, block, at):
    return lax.dynamic_update_index_in_dim(buffer, block, at, 0)


RING = (0, -1, 1, -2, 2, -3, 3, -4)


def gather_ring(block, axis):
    up, down, got = block, block, [block]
    for k in range(1, 5):
        up = lax.ppermute(up, axis, shift_table(8, 1))
        got.append(up)
        if k < 4:
            down = lax.ppermute(down, axis, shift_table(8, 7))
            got.append(down)
    return jnp.stack(got)


def scatter_ring(chunk, axis):
    up, down = chunk(4).astype(BF), chunk(5).astype(BF)
    for k in (3, 2, 1, 0):
        up = lax.ppermute(up, axis, shift_table(8, 1)).astype(F32)
        if k:
            up = (up + chunk(k)).astype(BF)
            down = lax.ppermute(down, axis, shift_table(8, 7)).astype(F32)
            if k > 1:
                down = (down + chunk(9 - k)).astype(BF)
    return chunk(0) + up + down


def scatter_swap(blocks, axis):
    got = lax.all_to_all(blocks, axis, 0, 0, tiled=True)
    return jnp.sum(got.astype(F32), axis=0)


def gather_shifts(block, axis, count, at):
    out = put(jnp.zeros((count,) + block.shape, block.dtype), block, at)
    for k in range(1, count):
        got = lax.ppermute(block, axis, shift_table(count, k))
        out = put(out, got, (at + count - k) % count)
    return out


def gathered_dot_kernel(squares, at, own, other, weight, out, x):
    step = pl.program_id(0)
    length, width = own.shape[2], own.shape[3]

    @pl.when(step == 0)
    def _():
        for slot, away in enumerate(RING):
            z = (at[0] + (away + 8)) & 7
            first = pl.multiple_of((z >> 1) * length, length)
            for h in range(2):
                for ref, core in ((own, at[1]), (other, 1 - at[1])):
                    column = pl.multiple_of((((z & 1) * 2 + h) * 2 + core) * width, width)
                    x[pl.ds(first, length), pl.ds(column, width)] = ref[slot, h]

    tile = weight.shape[1]
    here = pl.multiple_of(step * tile, tile)
    out[:, pl.ds(here, tile)] = jnp.dot(
        x[...], weight[...], preferred_element_type=F32
    ).astype(BF)

    if squares:

        @pl.when(step == pl.num_programs(0) - 1)
        def _():
            last = out.shape[1] - HD
            for first in range(0, x.shape[0], length):
                total = jnp.zeros((length, HD), F32)
                for column in range(0, x.shape[1], HD):
                    wide = x[first : first + length, column : column + HD].astype(F32)
                    total = total + wide * wide
                sums = jnp.sum(total, axis=1, keepdims=True)
                high = sums.astype(BF).astype(F32)
                lane = lax.broadcasted_iota(jnp.int32, (length, HD), 1)
                both = jnp.where(lane == 0, high, jnp.where(lane == 1, sums - high, 0.0))
                out[first : first + length, last:] = both.astype(BF)


def gathered_dot(at, own, other, weight, squares):
    _, _, length, width = own.shape
    depth, columns = weight.shape
    tokens = 32 * length * width // depth
    tile = 256 if columns % 256 == 0 else columns
    wide = columns + (HD if squares else 0)
    whole = lambda shape: pl.BlockSpec(shape, lambda i, at: (0,) * len(shape))
    return pl.pallas_call(
        functools.partial(gathered_dot_kernel, squares),
        out_shape=(
            jax.ShapeDtypeStruct((tokens, wide), BF),
            jax.ShapeDtypeStruct((tokens, depth), BF),
        ),
        grid_spec=pltpu.PrefetchScalarGridSpec(
            num_scalar_prefetch=1,
            grid=(columns // tile,),
            in_specs=[
                whole(own.shape),
                whole(other.shape),
                pl.BlockSpec((depth, tile), lambda i, at: (0, i)),
            ],
            out_specs=(whole((tokens, wide)), whole((tokens, depth))),
        ),
        compiler_params=pltpu.CompilerParams(vmem_limit_bytes=24 << 20),
        cost_estimate=pl.CostEstimate(
            flops=2 * tokens * depth * columns,
            bytes_accessed=2 * depth * (columns + 2 * tokens),
            transcendentals=0,
        ),
    )(at, own, other, weight)


def out_kernel(signs, at, *refs):
    out = refs[-1]
    count = len(signs)
    width = out.shape[3]
    for h in range(2):
        column = pl.multiple_of((h * 2 + at[1]) * width, width)
        total = None
        for sign, context, weight in zip(signs, refs[:count], refs[count:-1]):
            term = jnp.dot(
                context[...], weight[0, :, pl.ds(column, width)], preferred_element_type=F32
            )
            total = term * sign if total is None else total + term * sign
        out[0, h] = total.astype(out.dtype)


def out_blocks(at, contexts, weights, signs, kind):
    length, cols = contexts[0].shape
    depth = weights[0].shape[2]
    width = depth // 8
    return pl.pallas_call(
        functools.partial(out_kernel, signs),
        out_shape=jax.ShapeDtypeStruct((8, 2, length, width), kind),
        grid_spec=pltpu.PrefetchScalarGridSpec(
            num_scalar_prefetch=1,
            grid=(8,),
            in_specs=[pl.BlockSpec((length, cols), lambda i, at: (0, 0)) for _ in contexts]
            + [
                pl.BlockSpec(
                    (1, cols, depth // 2),
                    lambda i, at: (((at[0] + i) & 7) >> 1, 0, (at[0] + i) & 1),
                )
                for _ in weights
            ],
            out_specs=pl.BlockSpec((1, 2, length, width), lambda i, at: (i, 0, 0, 0)),
        ),
        compiler_params=pltpu.CompilerParams(vmem_limit_bytes=16 << 20),
        cost_estimate=pl.CostEstimate(
            flops=2 * len(signs) * length * cols * 16 * width,
            bytes_accessed=len(signs) * cols * depth * 8,
            transcendentals=0,
        ),
    )(at, *contexts, *weights)


def attend(queries, keys, values, keep):
    length = queries.shape[0]
    four = queries.reshape(length, -1, HD)
    scores = jnp.einsum("igd,jd->gij", four, keys, preferred_element_type=F32) * HD ** (-0.5)
    probs = jax.nn.softmax(jnp.where(keep, scores, -1e30), axis=-1)
    probs_b = probs.astype(BF)
    context = jnp.einsum("gij,jd->igd", probs_b, values, preferred_element_type=F32)
    return context.astype(BF).reshape(length, -1), probs, probs_b, four


def local(
    tokens, par_gain, par_wq, par_wk, par_wv, par_wo, var_wq, var_wk, var_wv, var_wo, lin_w, windows
):
    section = lax.axis_index("section")
    d = lax.axis_index("dp")
    z = lax.axis_index(Z)
    xh = lax.axis_index("xh")
    core = lax.axis_index("core")
    _, length, width = tokens.shape
    rows = par_wq.shape[1]
    cols = par_wq.shape[2]
    kv_cols = par_wk.shape[2]
    n_dp = lax.axis_size("dp")
    all_tokens = n_dp * length
    inv_scale = float(all_tokens) ** (-0.5)
    n_model = par_gain.shape[1]
    gain = lax.dynamic_slice_in_dim(par_gain[0], d * rows, rows, 0)
    positions = jnp.arange(length, dtype=jnp.int32)
    causal = positions[None, :] <= positions[:, None]
    windowed = causal & (positions[None, :] > positions[:, None] - windows[0])
    at_own = jnp.stack([z, core])
    at_other = jnp.stack([z, 1 - core])
    from_zero_own = jnp.stack([0 * z, core])
    from_zero_other = jnp.stack([0 * z, 1 - core])

    tok = tokens[0]
    tok_pair = ordered(turned(tok), turned(tok, 1), xh)

    par_o = lax.all_gather(par_wo[0], "dp", axis=0, tiled=False)
    stu_o = lax.all_gather(var_wo[0], "dp", axis=0, tiled=False)

    def gained(weight):
        return (weight[0].astype(F32) * gain[:, None]).astype(BF)

    def heads_weight(weight_q, weight_k, weight_v):
        own = jnp.stack([gained(weight_k).T, gained(weight_v).T])
        both = ordered(own, partner(own, "xh"), xh)
        four = ordered(both, partner(both, "core"), core)
        kv = four.transpose(2, 1, 0, 3, 4).reshape(2 * HD, rows)
        return jnp.concatenate([gained(weight_q), kv.T], axis=1)

    par_in = heads_weight(par_wq, par_wk, par_wv)
    stu_in = heads_weight(var_wq, var_wk, var_wv)
    both_in = jnp.concatenate([par_in, stu_in], axis=1)
    lin_in = gained(lin_w)
    stu_back = var_wo[0].T

    def scale_of(summed):
        mean = (summed[:, 0:1] + summed[:, 1:2]) / n_model
        return lax.rsqrt(mean + 1e-05)

    def cut(summed, scale):
        heads = (summed * scale).astype(BF)
        return heads[:, :cols], heads[:, cols : cols + HD], heads[:, cols + HD :]

    got = gather_ring(tok_pair, Z)
    part, _ = gathered_dot(at_own, got, partner(got, "core"), par_in, True)
    summed = scatter_swap(part.reshape(n_dp, length, -1), "dp")
    n_heads = cols + 2 * HD
    scale = scale_of(summed[:, n_heads:])
    context = attend(*cut(summed[:, :n_heads], scale), causal)[0]
    away = partner(out_blocks(at_other, [context], [par_o], (1.0,), BF), "core")
    here = out_blocks(at_own, [context], [par_o], (1.0,), F32)
    pair = scatter_ring(lambda k: here[k] + away[k].astype(F32), Z).astype(BF)
    to_next = [
        lax.ppermute(
            pair,
            ("section", "dp", "zh", "xh"),
            [(i, o + 32) for i, o in turn_table(flip)],
        )
        for flip in range(2)
    ]
    next_pair = tok_pair.astype(F32) + (to_next[0].astype(F32) + to_next[1].astype(F32))
    in_pair = jnp.where(section == 0, tok_pair, next_pair.astype(BF))

    got = gather_ring(in_pair, Z)
    part, x = gathered_dot(at_own, got, partner(got, "core"), both_in, True)
    summed = scatter_swap(part.reshape(n_dp, length, -1), "dp")
    scale = scale_of(summed[:, 2 * n_heads :])
    par_context = attend(*cut(summed[:, :n_heads], scale), causal)[0]
    queries, keys, values = cut(summed[:, n_heads : 2 * n_heads], scale)
    stu_context, probs, probs_b, query_four = attend(queries, keys, values, windowed)
    contexts, weights = [stu_context, par_context], [stu_o, par_o]
    away = partner(out_blocks(at_other, contexts, weights, (1.0, -1.0), BF), "core")
    here = out_blocks(at_own, contexts, weights, (1.0, -1.0), F32)
    pair = scatter_ring(lambda k: here[k] + away[k].astype(F32), Z).astype(BF)
    pair = turned(pair).astype(F32) + turned(pair, 1).astype(F32)
    grad_student = (pair * inv_scale).astype(BF)

    stu_all = gather_shifts(stu_context, "dp", n_dp, d).reshape(all_tokens, cols)
    later, x_later, _ = lax.optimization_barrier((par_context, x, here))
    away = partner(out_blocks(from_zero_other, [later], [par_o], (1.0,), BF), "core")
    here = out_blocks(from_zero_own, [later], [par_o], (1.0,), F32)
    target = lax.psum_scatter(
        (here + away.astype(F32)).astype(BF), Z, scatter_dimension=0, tiled=False
    )
    kept = lax.dynamic_index_in_dim(target, xh, 0, keepdims=False)
    sent = lax.dynamic_index_in_dim(target, 1 - xh, 0, keepdims=False)
    target = kept.astype(F32) + partner(sent, "xh").astype(F32)
    own_in = turned(lax.dynamic_index_in_dim(in_pair, xh, 0, keepdims=False))
    layer_out = (own_in.astype(F32) + target).astype(BF)
    linear = dot(x_later, lin_in, ((1,), (0,))).astype(BF)
    linear = scatter_swap(linear.reshape(n_dp, length, width), "dp")
    grad_linear = ((linear * scale - target) * inv_scale).astype(BF)
    grad_linear = (grad_linear.astype(F32) * scale).astype(BF)
    grad_linear = gather_shifts(grad_linear, "dp", n_dp, d).reshape(all_tokens, width)

    got = gather_ring(grad_student, Z)
    part, gs = gathered_dot(at_own, got, partner(got, "core"), stu_back, False)
    grad_context = scatter_swap(part.reshape(n_dp, length, cols), "dp").astype(BF)
    grad_four = grad_context.reshape(length, -1, HD)
    grad_probs = jnp.einsum("igd,jd->gij", grad_four, values, preferred_element_type=F32)
    grad_scores = probs * (grad_probs - jnp.sum(grad_probs * probs, axis=-1, keepdims=True))
    grad_scaled = (grad_scores * HD ** (-0.5)).astype(BF)
    grad_q = jnp.einsum("gij,jd->igd", grad_scaled, keys, preferred_element_type=F32)
    grad_q = (grad_q.reshape(length, cols) * scale).astype(BF)
    grad_k = jnp.einsum("gij,igd->dj", grad_scaled, query_four, preferred_element_type=F32)
    grad_v = jnp.einsum("gij,igd->dj", probs_b, grad_four, preferred_element_type=F32)
    members = HD // kv_cols
    parts = jnp.concatenate(
        [grad_k.reshape(members, kv_cols, length), grad_v.reshape(members, kv_cols, length)], axis=1
    )
    parts = (parts * scale.reshape(1, 1, length)).astype(BF)
    parts = jnp.broadcast_to(parts, (n_dp,) + parts.shape).reshape(-1, 2 * kv_cols, length)
    parts = lax.all_to_all(parts, ("dp", "xh", "core"), 0, 0, tiled=True)
    grad_q = gather_shifts(grad_q, "dp", n_dp, d).reshape(all_tokens, cols)
    grad_kv = parts.reshape(n_dp, members, 2 * kv_cols, length).astype(F32).sum(1).astype(BF)
    grad_kv = grad_kv.transpose(1, 0, 2).reshape(2 * kv_cols, all_tokens)

    over_tokens = ((0,), (0,))
    column = gain[:, None]
    grad_wq = dot(x, grad_q, over_tokens) * column
    grad_wkv = dot(x, grad_kv, ((0,), (1,))) * column
    grad_wo = dot(stu_all, gs, over_tokens)
    grad_lin = dot(x, grad_linear, over_tokens) * column
    return (
        layer_out[None, None],
        grad_wq[None],
        grad_wkv[None, :, :kv_cols],
        grad_wkv[None, :, kv_cols:],
        grad_wo[None],
        grad_lin[None],
    )


def solution(mesh):
    sizes = (mesh.shape["section"], mesh.shape["dp"], 4, 2, 2, 2)
    fine = Mesh(mesh.devices.reshape(sizes), ("section", "dp") + MP)
    by_columns = P("section", "dp", MP)
    by_rows = P("section", MP, "dp")
    return jax.shard_map(
        local,
        mesh=fine,
        in_specs=(
            P("dp", None, MP),
            P("section", None),
            by_columns,
            by_columns,
            by_columns,
            by_rows,
            by_columns,
            by_columns,
            by_columns,
            by_rows,
            by_columns,
            P("section"),
        ),
        out_specs=(
            P("section", "dp", None, MP),
            by_columns,
            by_columns,
            by_columns,
            by_rows,
            by_columns,
        ),
        check_vma=False,
    )
```

```python
import functools

import jax
import jax.numpy as jnp
from jax import lax
from jax.experimental import pallas as pl
from jax.experimental.pallas import tpu as pltpu
from jax.sharding import Mesh, PartitionSpec as P

HQ = 64
KVH = 8
HD = 128
MP = ("zh", "zl", "xh", "core")
Z = ("zh", "zl")
BF = jnp.bfloat16
F32 = jnp.float32


def dot(left, right, dims):
    return lax.dot_general(left, right, (dims, ((), ())), preferred_element_type=F32)


def shift_table(count, distance):
    return [(i, (i + distance) % count) for i in range(count)]


def ordered(own, other, at):
    return jnp.where(at == 0, jnp.stack([own, other]), jnp.stack([other, own]))


def partner(block, axis):
    return lax.ppermute(block, axis, [(0, 1), (1, 0)])


def turn_table(flip):
    return [
        ((a * 4 + b) * 2 + h, (b * 4 + a) * 2 + (h ^ flip))
        for a in range(4)
        for b in range(4)
        for h in range(2)
    ]


def turned(block, flip=0):
    return lax.ppermute(block, ("dp", "zh", "xh"), turn_table(flip))


def put(buffer, block, at):
    return lax.dynamic_update_index_in_dim(buffer, block, at, 0)


RING = (0, -1, 1, -2, 2, -3, 3, -4)


def gather_ring(block, axis):
    up, down, got = block, block, [block]
    for k in range(1, 5):
        up = lax.ppermute(up, axis, shift_table(8, 1))
        got.append(up)
        if k < 4:
            down = lax.ppermute(down, axis, shift_table(8, 7))
            got.append(down)
    return jnp.stack(got)


def scatter_ring(chunk, axis):
    up, down = chunk(4).astype(BF), chunk(5).astype(BF)
    for k in (3, 2, 1, 0):
        up = lax.ppermute(up, axis, shift_table(8, 1)).astype(F32)
        if k:
            up = (up + chunk(k)).astype(BF)
            down = lax.ppermute(down, axis, shift_table(8, 7)).astype(F32)
            if k > 1:
                down = (down + chunk(9 - k)).astype(BF)
    return chunk(0) + up + down


def scatter_dp(blocks, at):
    def block(k):
        return lax.dynamic_index_in_dim(blocks, (at + k) % 4, 0, keepdims=False)

    half = blocks.shape[1] // 2
    opposite = block(2)
    up = lax.ppermute(opposite[:half], "dp", shift_table(4, 1))
    down = lax.ppermute(opposite[half:], "dp", shift_table(4, 3))
    right, left = block(1), block(3)
    right = jnp.concatenate(
        [(right[:half].astype(F32) + up.astype(F32)).astype(BF), right[half:]], axis=0
    )
    left = jnp.concatenate(
        [left[:half], (left[half:].astype(F32) + down.astype(F32)).astype(BF)], axis=0
    )
    up = lax.ppermute(right, "dp", shift_table(4, 1))
    down = lax.ppermute(left, "dp", shift_table(4, 3))
    return block(0).astype(F32) + up.astype(F32) + down.astype(F32)


def gather_shifts(block, axis, count, at):
    out = put(jnp.zeros((count,) + block.shape, block.dtype), block, at)
    for k in range(1, count):
        got = lax.ppermute(block, axis, shift_table(count, k))
        out = put(out, got, (at + count - k) % count)
    return out


def in_kernel(wide_count, kv_count, squares, at, own, other, *refs):
    wides, kvs = refs[:wide_count], refs[wide_count : wide_count + kv_count]
    out, x, kv_rows = refs[wide_count + kv_count :]
    length, width = own.shape[2], own.shape[3]
    for slot, away in enumerate(RING):
        z = (at[0] + (away + 8)) & 7
        first = pl.multiple_of((z >> 1) * length, length)
        for h in range(2):
            for ref, core in ((own, at[1]), (other, 1 - at[1])):
                column = pl.multiple_of((((z & 1) * 2 + h) * 2 + core) * width, width)
                x[pl.ds(first, length), pl.ds(column, width)] = ref[slot, h]
    place = 0
    for weight in wides:
        tile = weight.shape[1]
        out[:, place : place + tile] = jnp.dot(
            x[...], weight[...], preferred_element_type=F32
        ).astype(BF)
        place += tile
    for kv in kvs:
        rows = kv.shape[2]
        for slot in range(4):
            h = (slot & 1) ^ at[2]
            core = (slot >> 1) ^ at[1]
            first = pl.multiple_of((h * 2 + core) * rows, rows)
            for which in range(2):
                kv_rows[pl.ds(first + which * 4 * rows, rows), :] = kv[slot, which]
        tile = 8 * rows
        out[:, place : place + tile] = lax.dot_general(
            x[...], kv_rows[...], (((1,), (1,)), ((), ())), preferred_element_type=F32
        ).astype(BF)
        place += tile
    if squares:
        for first in range(0, x.shape[0], length):
            total = jnp.zeros((length, HD), F32)
            for column in range(0, x.shape[1], HD):
                wide = x[first : first + length, column : column + HD].astype(F32)
                total = total + wide * wide
            sums = jnp.sum(total, axis=1, keepdims=True)
            high = sums.astype(BF).astype(F32)
            lane = lax.broadcasted_iota(jnp.int32, (length, HD), 1)
            both = jnp.where(lane == 0, high, jnp.where(lane == 1, sums - high, 0.0))
            out[first : first + length, place:] = both.astype(BF)


def gathered_dot(at, own, other, wides, kvs, squares):
    _, _, length, width = own.shape
    depth = wides[0].shape[0]
    tokens = 32 * length * width // depth
    columns = sum(w.shape[1] for w in wides) + sum(8 * kv.shape[2] for kv in kvs)
    wide = columns + (HD if squares else 0)
    kv_shape = (2 * HD, depth) if kvs else (16, HD)
    vmem = pl.BlockSpec(memory_space=pltpu.VMEM)
    return pl.pallas_call(
        functools.partial(in_kernel, len(wides), len(kvs), squares),
        out_shape=(
            jax.ShapeDtypeStruct((tokens, wide), BF),
            jax.ShapeDtypeStruct((tokens, depth), BF),
        ),
        in_specs=[pl.BlockSpec(memory_space=pltpu.SMEM)]
        + [vmem] * (2 + len(wides) + len(kvs)),
        out_specs=(vmem, vmem),
        scratch_shapes=[pltpu.VMEM(kv_shape, BF)],
        compiler_params=pltpu.CompilerParams(vmem_limit_bytes=32 << 20),
        cost_estimate=pl.CostEstimate(
            flops=2 * tokens * depth * columns,
            bytes_accessed=2 * depth * (columns + 2 * tokens),
            transcendentals=0,
        ),
    )(at, own, other, *wides, *kvs)


def out_kernel(at, contexts, *refs):
    out = refs[-1]
    weights = refs[:-1]
    tokens, cols = contexts.shape[-2:]
    length, width = out.shape[3:]
    for zl in range(2):
        for h in range(2):
            column = pl.multiple_of(((zl * 2 + h) * 2 + at[1]) * width, width)
            terms = [
                jnp.dot(
                    contexts[i], weight[:, pl.ds(column, width)], preferred_element_type=F32
                )
                for i, weight in enumerate(weights)
            ]
            if len(terms) == 2:
                terms[1] = terms[1] - terms[0]
            for zh in range(tokens // length):
                slot = (zh * 2 + zl + 8 - at[0]) & 7
                for i, term in enumerate(terms):
                    out[slot, i, h] = term[zh * length : (zh + 1) * length].astype(out.dtype)


def out_blocks(at, contexts, weights, length, kind):
    count, tokens, cols = contexts.shape
    depth = weights[0].shape[1]
    width = depth // 8
    vmem = pl.BlockSpec(memory_space=pltpu.VMEM)
    return pl.pallas_call(
        out_kernel,
        out_shape=jax.ShapeDtypeStruct((8, count, 2, length, width), kind),
        in_specs=[pl.BlockSpec(memory_space=pltpu.SMEM)] + [vmem] * (1 + count),
        out_specs=vmem,
        compiler_params=pltpu.CompilerParams(vmem_limit_bytes=24 << 20),
        cost_estimate=pl.CostEstimate(
            flops=count * tokens * cols * depth,
            bytes_accessed=count * (2 * cols * depth + 4 * tokens * depth),
            transcendentals=0,
        ),
    )(at, contexts, *weights)


def attend(queries, keys, values, keep):
    length = queries.shape[0]
    four = queries.reshape(length, -1, HD)
    scores = jnp.einsum("igd,jd->gij", four, keys, preferred_element_type=F32) * HD ** (-0.5)
    probs = jax.nn.softmax(jnp.where(keep, scores, -1e30), axis=-1)
    probs_b = probs.astype(BF)
    context = jnp.einsum("gij,jd->igd", probs_b, values, preferred_element_type=F32)
    return context.astype(BF).reshape(length, -1), probs, probs_b, four


def local(
    tokens, par_gain, par_wq, par_wk, par_wv, par_wo, var_wq, var_wk, var_wv, var_wo, lin_w, windows
):
    section = lax.axis_index("section")
    d = lax.axis_index("dp")
    z = lax.axis_index(Z)
    xh = lax.axis_index("xh")
    core = lax.axis_index("core")
    _, length, width = tokens.shape
    rows = par_wq.shape[1]
    cols = par_wq.shape[2]
    kv_cols = par_wk.shape[2]
    n_dp = lax.axis_size("dp")
    all_tokens = n_dp * length
    inv_scale = float(all_tokens) ** (-0.5)
    n_model = par_gain.shape[1]
    gain = lax.dynamic_slice_in_dim(par_gain[0], d * rows, rows, 0)
    positions = jnp.arange(length, dtype=jnp.int32)
    causal = positions[None, :] <= positions[:, None]
    windowed = causal & (positions[None, :] > positions[:, None] - windows[0])
    at_own = jnp.stack([z, core, xh])
    at_other = jnp.stack([z, 1 - core, xh])

    tok = tokens[0]
    tok_pair = ordered(turned(tok), turned(tok, 1), xh)

    def gained(weight):
        return (weight[0].astype(F32) * gain[:, None]).astype(BF)

    def kv_weight(weight_k, weight_v):
        own = jnp.stack([gained(weight_k).T, gained(weight_v).T])
        two = jnp.stack([own, partner(own, "xh")])
        return jnp.concatenate([two, partner(two, "core")])

    par_q = gained(par_wq)
    par_kv = kv_weight(par_wk, par_wv)
    stu_q = gained(var_wq)
    stu_kv = kv_weight(var_wk, var_wv)
    lin_in = gained(lin_w)
    stu_back = var_wo[0].T

    def scale_of(summed):
        mean = (summed[:, 0:1] + summed[:, 1:2]) / n_model
        return lax.rsqrt(mean + 1e-05)

    def cut(summed, scale, first):
        heads = (summed[:, first : first + cols + 2 * HD] * scale).astype(BF)
        return heads[:, :cols], heads[:, cols : cols + HD], heads[:, cols + HD :]

    def summed_out(contexts, weights):
        contexts = jnp.moveaxis(gather_shifts(contexts, "dp", n_dp, d), 1, 0)
        contexts = contexts.reshape(-1, all_tokens, cols)
        away = partner(out_blocks(at_other, contexts, weights, length, BF), "core")
        here = out_blocks(at_own, contexts, weights, length, F32)
        pair = scatter_ring(lambda k: here[k] + away[k].astype(F32), Z).astype(BF)
        return pair, contexts

    got = gather_ring(tok_pair, Z)
    part, _ = gathered_dot(at_own, got, partner(got, "core"), [par_q], [par_kv], True)
    summed = scatter_dp(part.reshape(n_dp, length, -1), d)
    scale = scale_of(summed[:, cols + 2 * HD :])
    context = attend(*cut(summed, scale, 0), causal)[0]
    pair, _ = summed_out(context[None], [par_wo[0]])
    pair = pair[0]
    to_next = [
        lax.ppermute(pair, ("section", "xh"), [(h, 2 + (h ^ flip)) for h in range(2)])
        for flip in range(2)
    ]
    next_pair = tok_pair.astype(F32) + (to_next[0].astype(F32) + to_next[1].astype(F32))
    in_pair = jnp.where(section == 0, tok_pair, next_pair.astype(BF))

    got = gather_ring(in_pair, Z)
    part, x = gathered_dot(
        at_own, got, partner(got, "core"), [par_q, stu_q, lin_in], [par_kv, stu_kv], True
    )
    summed = scatter_dp(part.reshape(n_dp, length, -1), d)
    kv_first = 2 * cols + width
    scale = scale_of(summed[:, kv_first + 4 * HD :])
    heads = jnp.concatenate(
        [
            summed[:, :cols],
            summed[:, kv_first : kv_first + 2 * HD],
            summed[:, cols : 2 * cols],
            summed[:, kv_first + 2 * HD : kv_first + 4 * HD],
        ],
        axis=1,
    )
    linear = summed[:, 2 * cols : kv_first] * scale
    par_context = attend(*cut(heads, scale, 0), causal)[0]
    queries, keys, values = cut(heads, scale, cols + 2 * HD)
    stu_context, probs, probs_b, query_four = attend(queries, keys, values, windowed)
    pair, contexts = summed_out(
        jnp.stack([par_context, stu_context]), [par_wo[0], var_wo[0]]
    )
    stu_all = contexts[1]
    pair = pair.astype(F32) + partner(pair, "xh").astype(F32)
    target, above = pair[0], pair[1]
    grad_student = (above * inv_scale).astype(BF)
    got = gather_ring(grad_student, Z)

    own_target = lax.dynamic_index_in_dim(target, xh, 0, keepdims=False)
    own_in = lax.dynamic_index_in_dim(in_pair, xh, 0, keepdims=False)
    own_out = (own_in.astype(F32) + own_target).astype(BF)
    back = turned(jnp.stack([own_out, own_target.astype(BF)]))
    layer_out = back[0]
    grad_linear = ((linear - back[1].astype(F32)) * inv_scale).astype(BF)
    grad_linear = (grad_linear.astype(F32) * scale).astype(BF)
    grad_linear = gather_shifts(grad_linear, "dp", n_dp, d).reshape(all_tokens, width)

    part, gs = gathered_dot(at_own, got, partner(got, "core"), [stu_back], [], False)
    grad_context = scatter_dp(part.reshape(n_dp, length, cols), d).astype(BF)
    grad_four = grad_context.reshape(length, -1, HD)
    grad_probs = jnp.einsum("igd,jd->gij", grad_four, values, preferred_element_type=F32)
    grad_scores = probs * (grad_probs - jnp.sum(grad_probs * probs, axis=-1, keepdims=True))
    grad_scaled = (grad_scores * HD ** (-0.5)).astype(BF)
    grad_q = jnp.einsum("gij,jd->igd", grad_scaled, keys, preferred_element_type=F32)
    grad_q = (grad_q.reshape(length, cols) * scale).astype(BF)
    grad_k = jnp.einsum("gij,igd->dj", grad_scaled, query_four, preferred_element_type=F32)
    grad_v = jnp.einsum("gij,igd->dj", probs_b, grad_four, preferred_element_type=F32)
    members = HD // kv_cols
    parts = jnp.concatenate(
        [grad_k.reshape(members, kv_cols, length), grad_v.reshape(members, kv_cols, length)], axis=1
    )
    parts = (parts * scale.reshape(1, 1, length)).astype(BF)
    parts = jnp.broadcast_to(parts, (n_dp,) + parts.shape).reshape(-1, 2 * kv_cols, length)
    parts = lax.all_to_all(parts, ("dp", "xh", "core"), 0, 0, tiled=True)
    grad_q = gather_shifts(grad_q, "dp", n_dp, d).reshape(all_tokens, cols)
    grad_kv = parts.reshape(n_dp, members, 2 * kv_cols, length).astype(F32).sum(1).astype(BF)
    grad_kv = grad_kv.transpose(1, 0, 2).reshape(2 * kv_cols, all_tokens)

    over_tokens = ((0,), (0,))
    column = gain[:, None]
    grad_wq = dot(x, grad_q, over_tokens) * column
    grad_wkv = dot(x, grad_kv, ((0,), (1,))) * column
    grad_wo = dot(stu_all, gs, over_tokens)
    grad_lin = dot(x, grad_linear, over_tokens) * column
    return (
        layer_out[None, None],
        grad_wq[None],
        grad_wkv[None, :, :kv_cols],
        grad_wkv[None, :, kv_cols:],
        grad_wo[None],
        grad_lin[None],
    )


def solution(mesh):
    sizes = (mesh.shape["section"], mesh.shape["dp"], 4, 2, 2, 2)
    fine = Mesh(mesh.devices.reshape(sizes), ("section", "dp") + MP)
    by_columns = P("section", "dp", MP)
    by_rows = P("section", MP, "dp")
    return jax.shard_map(
        local,
        mesh=fine,
        in_specs=(
            P("dp", None, MP),
            P("section", None),
            by_columns,
            by_columns,
            by_columns,
            by_rows,
            by_columns,
            by_columns,
            by_columns,
            by_rows,
            by_columns,
            P("section"),
        ),
        out_specs=(
            P("section", "dp", None, MP),
            by_columns,
            by_columns,
            by_columns,
            by_rows,
            by_columns,
        ),
        check_vma=False,
    )
```

```python
import functools

import jax
import jax.numpy as jnp
from jax import lax
from jax.experimental import pallas as pl
from jax.experimental.pallas import tpu as pltpu
from jax.sharding import Mesh, PartitionSpec as P

HQ = 64
KVH = 8
HD = 128
MP = ("zh", "zl", "xh", "core")
Z = ("zh", "zl")
BF = jnp.bfloat16
F32 = jnp.float32


def dot(left, right, dims):
    return lax.dot_general(left, right, (dims, ((), ())), preferred_element_type=F32)


def shift_table(count, distance):
    return [(i, (i + distance) % count) for i in range(count)]


def ordered(own, other, at):
    return jnp.where(at == 0, jnp.stack([own, other]), jnp.stack([other, own]))


def partner(block, axis):
    return lax.ppermute(block, axis, [(0, 1), (1, 0)])


def turn_table(flip):
    return [
        ((a * 4 + b) * 2 + h, (b * 4 + a) * 2 + (h ^ flip))
        for a in range(4)
        for b in range(4)
        for h in range(2)
    ]


def turned(block, flip=0):
    return lax.ppermute(block, ("dp", "zh", "xh"), turn_table(flip))


def put(buffer, block, at):
    return lax.dynamic_update_index_in_dim(buffer, block, at, 0)


RING = (0, -1, 1, -2, 2, -3, 3, -4)


def gather_ring(block, axis, beside=(), by=3):
    up, down, got = block, block, [block]
    for k in range(1, 5):
        if k == by and beside:
            up, down, *beside = lax.optimization_barrier((up, down, *beside))
        up = lax.ppermute(up, axis, shift_table(8, 1))
        got.append(up)
        if k < 4:
            down = lax.ppermute(down, axis, shift_table(8, 7))
            got.append(down)
    return jnp.stack(got), beside


def scatter_ring(chunk, axis):
    up, down = chunk(4).astype(BF), chunk(5).astype(BF)
    for k in (3, 2, 1, 0):
        up = lax.ppermute(up, axis, shift_table(8, 1)).astype(F32)
        if k:
            up = (up + chunk(k)).astype(BF)
            down = lax.ppermute(down, axis, shift_table(8, 7)).astype(F32)
            if k > 1:
                down = (down + chunk(9 - k)).astype(BF)
    return chunk(0) + up + down


def scatter_dp(blocks, at):
    def block(k):
        return lax.dynamic_index_in_dim(blocks, (at + k) % 4, 0, keepdims=False)

    got = [lax.ppermute(block(k), "dp", shift_table(4, k)) for k in (2, 1, 3)]
    total = block(0).astype(F32)
    for one in got:
        total = total + one.astype(F32)
    return total


def gather_shifts(block, axis, count, at):
    out = put(jnp.zeros((count,) + block.shape, block.dtype), block, at)
    for k in range(1, count):
        got = lax.ppermute(block, axis, shift_table(count, k))
        out = put(out, got, (at + count - k) % count)
    return out


def in_kernel(wide_count, kv_count, squares, at, own, other, *refs):
    wides, kvs = refs[:wide_count], refs[wide_count : wide_count + kv_count]
    out, x, *aside, kv_rows = refs[wide_count + kv_count :]
    length, width = own.shape[2], own.shape[3]
    for slot, away in enumerate(RING):
        z = (at[0] + (away + 8)) & 7
        first = pl.multiple_of((z >> 1) * length, length)
        for h in range(2):
            for ref, core in ((own, at[1]), (other, 1 - at[1])):
                column = pl.multiple_of((((z & 1) * 2 + h) * 2 + core) * width, width)
                x[pl.ds(first, length), pl.ds(column, width)] = ref[slot, h]
    place = 0
    if aside:
        aside[0][...] = jnp.dot(x[...], wides[-1][...], preferred_element_type=F32).astype(BF)
    for weight in wides[: wide_count - len(aside)]:
        tile = weight.shape[1]
        out[:, place : place + tile] = jnp.dot(
            x[...], weight[...], preferred_element_type=F32
        ).astype(BF)
        place += tile
    for kv in kvs:
        rows = kv.shape[2]
        for slot in range(4):
            h = (slot & 1) ^ at[2]
            core = (slot >> 1) ^ at[1]
            first = pl.multiple_of((h * 2 + core) * rows, rows)
            for which in range(2):
                kv_rows[pl.ds(first + which * 4 * rows, rows), :] = kv[slot, which]
        tile = 8 * rows
        out[:, place : place + tile] = lax.dot_general(
            x[...], kv_rows[...], (((1,), (1,)), ((), ())), preferred_element_type=F32
        ).astype(BF)
        place += tile
    if squares:
        for first in range(0, x.shape[0], length):
            total = jnp.zeros((length, HD), F32)
            for column in range(0, x.shape[1], HD):
                wide = x[first : first + length, column : column + HD].astype(F32)
                total = total + wide * wide
            sums = jnp.sum(total, axis=1, keepdims=True)
            high = sums.astype(BF).astype(F32)
            lane = lax.broadcasted_iota(jnp.int32, (length, HD), 1)
            both = jnp.where(lane == 0, high, jnp.where(lane == 1, sums - high, 0.0))
            out[first : first + length, place:] = both.astype(BF)


def gathered_dot(at, own, other, wides, kvs, squares, aside=()):
    _, _, length, width = own.shape
    depth = wides[0].shape[0]
    tokens = 32 * length * width // depth
    columns = sum(w.shape[1] for w in wides) + sum(8 * kv.shape[2] for kv in kvs)
    wide = columns + (HD if squares else 0)
    kv_shape = (2 * HD, depth) if kvs else (16, HD)
    vmem = pl.BlockSpec(memory_space=pltpu.VMEM)
    return pl.pallas_call(
        functools.partial(in_kernel, len(wides) + len(aside), len(kvs), squares),
        out_shape=(
            jax.ShapeDtypeStruct((tokens, wide), BF),
            jax.ShapeDtypeStruct((tokens, depth), BF),
        )
        + tuple(jax.ShapeDtypeStruct((tokens, w.shape[1]), BF) for w in aside),
        in_specs=[pl.BlockSpec(memory_space=pltpu.SMEM)]
        + [vmem] * (2 + len(wides) + len(aside) + len(kvs)),
        out_specs=(vmem, vmem) + (vmem,) * len(aside),
        scratch_shapes=[pltpu.VMEM(kv_shape, BF)],
        compiler_params=pltpu.CompilerParams(vmem_limit_bytes=32 << 20),
        cost_estimate=pl.CostEstimate(
            flops=2 * tokens * depth * columns,
            bytes_accessed=2 * depth * (columns + 2 * tokens),
            transcendentals=0,
        ),
    )(at, own, other, *wides, *aside, *kvs)


def out_kernel(at, contexts, *refs):
    out = refs[-1]
    weights = refs[:-1]
    tokens, cols = contexts.shape[-2:]
    length, width = out.shape[3:]
    for zl in range(2):
        for h in range(2):
            column = pl.multiple_of(((zl * 2 + h) * 2 + at[1]) * width, width)
            terms = [
                jnp.dot(
                    contexts[i], weight[:, pl.ds(column, width)], preferred_element_type=F32
                )
                for i, weight in enumerate(weights)
            ]
            if len(terms) == 2:
                terms[1] = terms[1] - terms[0]
            for zh in range(tokens // length):
                slot = (zh * 2 + zl + 8 - at[0]) & 7
                for i, term in enumerate(terms):
                    out[slot, i, h] = term[zh * length : (zh + 1) * length].astype(out.dtype)


def out_blocks(at, contexts, weights, length, kind):
    count, tokens, cols = contexts.shape
    depth = weights[0].shape[1]
    width = depth // 8
    vmem = pl.BlockSpec(memory_space=pltpu.VMEM)
    return pl.pallas_call(
        out_kernel,
        out_shape=jax.ShapeDtypeStruct((8, count, 2, length, width), kind),
        in_specs=[pl.BlockSpec(memory_space=pltpu.SMEM)] + [vmem] * (1 + count),
        out_specs=vmem,
        compiler_params=pltpu.CompilerParams(vmem_limit_bytes=24 << 20),
        cost_estimate=pl.CostEstimate(
            flops=count * tokens * cols * depth,
            bytes_accessed=count * (2 * cols * depth + 4 * tokens * depth),
            transcendentals=0,
        ),
    )(at, contexts, *weights)


def attend(queries, keys, values, keep):
    length = queries.shape[0]
    four = queries.reshape(length, -1, HD)
    scores = jnp.einsum("igd,jd->gij", four, keys, preferred_element_type=F32) * HD ** (-0.5)
    probs = jax.nn.softmax(jnp.where(keep, scores, -1e30), axis=-1)
    probs_b = probs.astype(BF)
    context = jnp.einsum("gij,jd->igd", probs_b, values, preferred_element_type=F32)
    return context.astype(BF).reshape(length, -1), probs, probs_b, four


def local(
    tokens, par_gain, par_wq, par_wk, par_wv, par_wo, var_wq, var_wk, var_wv, var_wo, lin_w, windows
):
    section = lax.axis_index("section")
    d = lax.axis_index("dp")
    z = lax.axis_index(Z)
    xh = lax.axis_index("xh")
    core = lax.axis_index("core")
    _, length, width = tokens.shape
    rows = par_wq.shape[1]
    cols = par_wq.shape[2]
    kv_cols = par_wk.shape[2]
    n_dp = lax.axis_size("dp")
    all_tokens = n_dp * length
    inv_scale = float(all_tokens) ** (-0.5)
    n_model = par_gain.shape[1]
    gain = lax.dynamic_slice_in_dim(par_gain[0], d * rows, rows, 0)
    positions = jnp.arange(length, dtype=jnp.int32)
    causal = positions[None, :] <= positions[:, None]
    windowed = causal & (positions[None, :] > positions[:, None] - windows[0])
    at_own = jnp.stack([z, core, xh])
    at_other = jnp.stack([z, 1 - core, xh])

    tok = tokens[0]
    tok_pair = ordered(turned(tok), turned(tok, 1), xh)

    def gained(weight):
        return (weight[0].astype(F32) * gain[:, None]).astype(BF)

    def kv_weight(weight_k, weight_v):
        own = jnp.stack([gained(weight_k).T, gained(weight_v).T])
        two = jnp.stack([own, partner(own, "xh")])
        return jnp.concatenate([two, partner(two, "core")])

    par_q = gained(par_wq)
    par_kv = kv_weight(par_wk, par_wv)
    stu_q = gained(var_wq)
    stu_kv = kv_weight(var_wk, var_wv)
    lin_in = gained(lin_w)
    stu_back = var_wo[0].T

    def scale_of(summed):
        mean = (summed[:, 0:1] + summed[:, 1:2]) / n_model
        return lax.rsqrt(mean + 1e-05)

    def cut(summed, scale, first):
        heads = (summed[:, first : first + cols + 2 * HD] * scale).astype(BF)
        return heads[:, :cols], heads[:, cols : cols + HD], heads[:, cols + HD :]

    def summed_out(contexts, weights):
        contexts = jnp.moveaxis(gather_shifts(contexts, "dp", n_dp, d), 1, 0)
        contexts = contexts.reshape(-1, all_tokens, cols)
        away = partner(out_blocks(at_other, contexts, weights, length, BF), "core")
        here = out_blocks(at_own, contexts, weights, length, F32)
        pair = scatter_ring(lambda k: here[k] + away[k].astype(F32), Z).astype(BF)
        return pair, contexts

    got, (par_q, par_kv) = gather_ring(tok_pair, Z, (par_q, par_kv))
    part, _ = gathered_dot(at_own, got, partner(got, "core"), [par_q], [par_kv], True)
    summed = scatter_dp(part.reshape(n_dp, length, -1), d)
    scale = scale_of(summed[:, cols + 2 * HD :])
    context = attend(*cut(summed, scale, 0), causal)[0]
    pair, _ = summed_out(context[None], [par_wo[0]])
    pair = pair[0]
    to_next = [
        lax.ppermute(pair, ("section", "xh"), [(h, 2 + (h ^ flip)) for h in range(2)])
        for flip in range(2)
    ]
    next_pair = tok_pair.astype(F32) + (to_next[0].astype(F32) + to_next[1].astype(F32))
    in_pair = jnp.where(section == 0, tok_pair, next_pair.astype(BF))

    got, (stu_q, stu_kv, lin_in, stu_back) = gather_ring(
        in_pair, Z, (stu_q, stu_kv, lin_in, stu_back)
    )
    part, x, linear = gathered_dot(
        at_own, got, partner(got, "core"), [par_q, stu_q], [par_kv, stu_kv], True, [lin_in]
    )
    summed = scatter_dp(part.reshape(n_dp, length, -1), d)
    linear = lax.psum_scatter(linear, "dp", scatter_dimension=0, tiled=True)
    kv_first = 2 * cols
    scale = scale_of(summed[:, kv_first + 4 * HD :])
    heads = jnp.concatenate(
        [
            summed[:, :cols],
            summed[:, kv_first : kv_first + 2 * HD],
            summed[:, cols : 2 * cols],
            summed[:, kv_first + 2 * HD : kv_first + 4 * HD],
        ],
        axis=1,
    )
    par_context = attend(*cut(heads, scale, 0), causal)[0]
    queries, keys, values = cut(heads, scale, cols + 2 * HD)
    stu_context, probs, probs_b, query_four = attend(queries, keys, values, windowed)
    pair, contexts = summed_out(
        jnp.stack([par_context, stu_context]), [par_wo[0], var_wo[0]]
    )
    stu_all = contexts[1]
    pair = pair.astype(F32) + partner(pair, "xh").astype(F32)
    target, above = pair[0], pair[1]
    grad_student = (above * inv_scale).astype(BF)

    own_target = lax.dynamic_index_in_dim(target, xh, 0, keepdims=False)
    own_in = lax.dynamic_index_in_dim(in_pair, xh, 0, keepdims=False)
    own_out = (own_in.astype(F32) + own_target).astype(BF)
    back = turned(jnp.stack([own_out, own_target.astype(BF)]))
    grad_linear = linear.astype(F32) * scale - back[1].astype(F32)
    grad_linear = (grad_linear * inv_scale).astype(BF)
    grad_linear = (grad_linear.astype(F32) * scale).astype(BF)
    layer_out = back[0]
    got, (grad_linear, layer_out) = gather_ring(grad_student, Z, (grad_linear, layer_out), 4)

    part, gs = gathered_dot(at_own, got, partner(got, "core"), [stu_back], [], False)
    grad_context = scatter_dp(part.reshape(n_dp, length, cols), d).astype(BF)
    grad_four = grad_context.reshape(length, -1, HD)
    grad_probs = jnp.einsum("igd,jd->gij", grad_four, values, preferred_element_type=F32)
    grad_scores = probs * (grad_probs - jnp.sum(grad_probs * probs, axis=-1, keepdims=True))
    grad_scaled = (grad_scores * HD ** (-0.5)).astype(BF)
    grad_q = jnp.einsum("gij,jd->igd", grad_scaled, keys, preferred_element_type=F32)
    grad_q = (grad_q.reshape(length, cols) * scale).astype(BF)
    grad_k = jnp.einsum("gij,igd->dj", grad_scaled, query_four, preferred_element_type=F32)
    grad_v = jnp.einsum("gij,igd->dj", probs_b, grad_four, preferred_element_type=F32)
    members = HD // kv_cols
    parts = jnp.concatenate(
        [grad_k.reshape(members, kv_cols, length), grad_v.reshape(members, kv_cols, length)], axis=1
    )
    parts = (parts * scale.reshape(1, 1, length)).astype(BF)
    parts = jnp.broadcast_to(parts, (n_dp,) + parts.shape).reshape(-1, 2 * kv_cols, length)
    parts = lax.all_to_all(parts, ("dp", "xh", "core"), 0, 0, tiled=True)
    gathered = gather_shifts(jnp.concatenate([grad_q, grad_linear], axis=1), "dp", n_dp, d)
    gathered = gathered.reshape(all_tokens, cols + width)
    grad_q, grad_linear = gathered[:, :cols], gathered[:, cols:]
    grad_kv = parts.reshape(n_dp, members, 2 * kv_cols, length).astype(F32).sum(1).astype(BF)
    grad_kv = grad_kv.transpose(1, 0, 2).reshape(2 * kv_cols, all_tokens)

    over_tokens = ((0,), (0,))
    column = gain[:, None]
    grad_wq = dot(x, grad_q, over_tokens) * column
    grad_wkv = dot(x, grad_kv, ((0,), (1,))) * column
    grad_wo = dot(stu_all, gs, over_tokens)
    grad_lin = dot(x, grad_linear, over_tokens) * column
    return (
        layer_out[None, None],
        grad_wq[None],
        grad_wkv[None, :, :kv_cols],
        grad_wkv[None, :, kv_cols:],
        grad_wo[None],
        grad_lin[None],
    )


def solution(mesh):
    sizes = (mesh.shape["section"], mesh.shape["dp"], 4, 2, 2, 2)
    fine = Mesh(mesh.devices.reshape(sizes), ("section", "dp") + MP)
    by_columns = P("section", "dp", MP)
    by_rows = P("section", MP, "dp")
    return jax.shard_map(
        local,
        mesh=fine,
        in_specs=(
            P("dp", None, MP),
            P("section", None),
            by_columns,
            by_columns,
            by_columns,
            by_rows,
            by_columns,
            by_columns,
            by_columns,
            by_rows,
            by_columns,
            P("section"),
        ),
        out_specs=(
            P("section", "dp", None, MP),
            by_columns,
            by_columns,
            by_columns,
            by_rows,
            by_columns,
        ),
        check_vma=False,
    )
```

```python
import functools

import jax
import jax.numpy as jnp
from jax import lax
from jax.experimental import pallas as pl
from jax.experimental.pallas import tpu as pltpu
from jax.sharding import Mesh, PartitionSpec as P

HQ = 64
KVH = 8
HD = 128
MP = ("zh", "zl", "xh", "core")
Z = ("zh", "zl")
BF = jnp.bfloat16
F32 = jnp.float32


def dot(left, right, dims):
    return lax.dot_general(left, right, (dims, ((), ())), preferred_element_type=F32)


def shift_table(count, distance):
    return [(i, (i + distance) % count) for i in range(count)]


def ordered(own, other, at):
    return jnp.where(at == 0, jnp.stack([own, other]), jnp.stack([other, own]))


def partner(block, axis):
    return lax.ppermute(block, axis, [(0, 1), (1, 0)])


def turn_table(flip):
    return [
        ((a * 4 + b) * 2 + h, (b * 4 + a) * 2 + (h ^ flip))
        for a in range(4)
        for b in range(4)
        for h in range(2)
    ]


def turned(block, flip=0):
    return lax.ppermute(block, ("dp", "zh", "xh"), turn_table(flip))


def ahead(block, hops):
    table = []
    for z in range(8):
        table.append((z * 2, (z + hops) % 8 * 2))
        table.append((z * 2 + 1, (z - hops) % 8 * 2 + 1))
    return lax.ppermute(block, Z + ("core",), table)


def gather_z(pair, beside=()):
    quad = jnp.stack([pair, partner(pair, "core")])
    one = ahead(quad, 1)
    two = ahead(quad, 2)
    if beside:
        two, *beside = lax.optimization_barrier((two, *beside))
    three = ahead(two, 1)
    four = ahead(two[0], 2)
    mine = [one, two, three, four]
    theirs = [partner(block, "core") for block in mine]
    return (quad, mine, theirs), beside


def scatter_z(first, rest):
    s3, s4 = first(0, 2).astype(BF), first(2, 3)[0].astype(BF)
    s1 = rest(0, 2).astype(BF)
    three = ahead(s3, 1)
    four = ahead(s4, 2)
    one = ahead(s1, 1)
    s2 = rest(2, 4) + three.astype(F32)
    s2 = jnp.stack([s2[0] + four.astype(F32), s2[1]]).astype(BF)
    two = ahead(s2, 2)
    total = one.astype(F32) + two.astype(F32)
    across = partner(total[1].astype(BF), "core")
    return rest(4, 5)[0] + total[0] + across.astype(F32)


def scatter_dp(blocks):
    got = [lax.ppermute(blocks[k], "dp", shift_table(4, k)) for k in (2, 1, 3)]
    return [blocks[0]] + got


def summed(blocks):
    total = blocks[0].astype(F32)
    for block in blocks[1:]:
        total = total + block.astype(F32)
    return total


def gather_dp(block):
    got = {k: lax.ppermute(block, "dp", shift_table(4, 4 - k)) for k in (2, 1, 3)}
    return [block, got[1], got[2], got[3]]


def in_kernel(counts, squares, at, quad, *refs):
    mine, theirs, refs = refs[:4], refs[4:8], refs[8:]
    weights, refs = refs[: counts[0]], refs[counts[0] :]
    sides, refs = refs[: counts[1]], refs[counts[1] :]
    kvs, refs = refs[: counts[2]], refs[counts[2] :]
    outs, x, asides, kv_rows = refs[:4], refs[4], refs[5:-1], refs[-1]
    length, width = quad.shape[2], quad.shape[3]
    z0, core, xh, d = at[0], at[1], at[2], at[3]
    up = 2 * core - 1

    def place(block, z, feature_core):
        z = (z + 8) & 7
        first = pl.multiple_of((((z >> 1) - d) & 3) * length, length)
        for h in range(2):
            column = pl.multiple_of((((z & 1) * 2 + h) * 2 + feature_core) * width, width)
            x[pl.ds(first, length), pl.ds(column, width)] = block[h]

    for i in range(2):
        place(quad.at[i], z0, core ^ i)
    for hops in range(1, 4):
        for i in range(2):
            place(mine[hops - 1].at[i], z0 + up * hops, core ^ i)
            place(theirs[hops - 1].at[i], z0 - up * hops, core ^ i ^ 1)
    place(mine[3], z0 + 4, core)
    place(theirs[3], z0 + 4, core ^ 1)

    column = 0

    def put(product):
        for k in range(4):
            outs[k][:, column : column + product.shape[1]] = product[
                k * length : (k + 1) * length
            ].astype(BF)

    for weight in weights:
        put(jnp.dot(x[...], weight[...], preferred_element_type=F32))
        column += weight.shape[1]
    for kv in kvs:
        rows = kv.shape[2]
        for slot in range(4):
            member = ((slot & 1) ^ xh) * 2 + ((slot >> 1) ^ core)
            first = pl.multiple_of(member * rows, rows)
            for which in range(2):
                kv_rows[pl.ds(first + which * 4 * rows, rows), :] = kv[slot, which]
        put(
            lax.dot_general(
                x[...], kv_rows[...], (((1,), (1,)), ((), ())), preferred_element_type=F32
            )
        )
        column += 8 * rows
    if squares:
        for k in range(4):
            total = jnp.zeros((length, HD), F32)
            for lane in range(0, x.shape[1], HD):
                wide = x[k * length : (k + 1) * length, lane : lane + HD].astype(F32)
                total = total + wide * wide
            sums = jnp.sum(total, axis=1, keepdims=True)
            high = sums.astype(BF).astype(F32)
            lane = lax.broadcasted_iota(jnp.int32, (length, HD), 1)
            both = jnp.where(lane == 0, high, jnp.where(lane == 1, sums - high, 0.0))
            outs[k][:, column:] = both.astype(BF)
    for weight, aside in zip(sides, asides):
        product = jnp.dot(x[...], weight[...], preferred_element_type=F32).astype(BF)
        for k in range(4):
            first = pl.multiple_of(((k + d) & 3) * length, length)
            aside[pl.ds(first, length), :] = product[k * length : (k + 1) * length]


def gathered_dot(at, gathered, weights, kvs, squares, sides=()):
    quad, mine, theirs = gathered
    length, width = quad.shape[2:]
    depth = weights[0].shape[0]
    tokens = 4 * length
    columns = sum(w.shape[1] for w in weights) + sum(8 * kv.shape[2] for kv in kvs)
    wide = columns + (HD if squares else 0)
    kv_shape = (2 * HD, depth) if kvs else (16, HD)
    vmem = pl.BlockSpec(memory_space=pltpu.VMEM)
    operands = [quad, *mine, *theirs, *weights, *sides, *kvs]
    shapes = [(length, wide)] * 4 + [(tokens, depth)] + [(tokens, w.shape[1]) for w in sides]
    out = pl.pallas_call(
        functools.partial(in_kernel, (len(weights), len(sides), len(kvs)), squares),
        out_shape=tuple(jax.ShapeDtypeStruct(shape, BF) for shape in shapes),
        in_specs=[pl.BlockSpec(memory_space=pltpu.SMEM)] + [vmem] * len(operands),
        out_specs=(vmem,) * len(shapes),
        scratch_shapes=[pltpu.VMEM(kv_shape, BF)],
        compiler_params=pltpu.CompilerParams(vmem_limit_bytes=32 << 20),
        cost_estimate=pl.CostEstimate(
            flops=2 * tokens * depth * columns,
            bytes_accessed=2 * depth * (columns + 2 * tokens),
            transcendentals=0,
        ),
    )(at, *operands)
    return out[:4], out[4], out[5:]


FIRST = ((3, 0), (3, 1), (4, 0))
REST = ((1, 0), (1, 1), (2, 0), (2, 1), (0, 0))


def out_kernel(count, at, *refs):
    contexts, weights = refs[:4], refs[4 : 4 + count]
    outs, rows = refs[4 + count : 8 + count], refs[8 + count]
    length, width = outs[0].shape[3:]
    z0, own_core, d = at[0], at[1], at[3]
    for k in range(4):
        rows[k] = contexts[k][...]
    for out, units, core in (
        (outs[0], FIRST, 1 - own_core),
        (outs[1], REST, 1 - own_core),
        (outs[2], FIRST, own_core),
        (outs[3], REST, own_core),
    ):
        for unit, (hops, other) in enumerate(units):
            z = (z0 + (1 - 2 * core) * hops + 8) & 7
            k = ((z >> 1) - d) & 3
            for h in range(2):
                column = (((z & 1) * 2 + h) * 2 + (core ^ other)) * width
                column = pl.multiple_of(column, width)
                terms = [
                    jnp.dot(
                        rows[k, i], weight[:, pl.ds(column, width)], preferred_element_type=F32
                    )
                    for i, weight in enumerate(weights)
                ]
                if count == 2:
                    terms[1] = terms[1] - terms[0]
                for i, term in enumerate(terms):
                    out[unit, i, h] = term.astype(out.dtype)


def out_blocks(at, contexts, weights):
    count, length, cols = contexts[0].shape
    depth = weights[0].shape[1]
    width = depth // 8
    vmem = pl.BlockSpec(memory_space=pltpu.VMEM)
    unit = (count, 2, length, width)
    return pl.pallas_call(
        functools.partial(out_kernel, count),
        out_shape=tuple(
            jax.ShapeDtypeStruct((len(units),) + unit, kind)
            for kind in (BF, F32)
            for units in (FIRST, REST)
        ),
        in_specs=[pl.BlockSpec(memory_space=pltpu.SMEM)] + [vmem] * (4 + count),
        out_specs=(vmem,) * 4,
        scratch_shapes=[pltpu.VMEM((4, count, length, cols), BF)],
        compiler_params=pltpu.CompilerParams(vmem_limit_bytes=24 << 20),
        cost_estimate=pl.CostEstimate(
            flops=8 * count * length * cols * depth,
            bytes_accessed=count * (2 * cols * depth + 24 * length * depth),
            transcendentals=0,
        ),
    )(at, *contexts, *weights)


def attend(queries, keys, values, keep):
    length = queries.shape[0]
    four = queries.reshape(length, -1, HD)
    scores = jnp.einsum("igd,jd->gij", four, keys, preferred_element_type=F32) * HD ** (-0.5)
    probs = jax.nn.softmax(jnp.where(keep, scores, -1e30), axis=-1)
    probs_b = probs.astype(BF)
    context = jnp.einsum("gij,jd->igd", probs_b, values, preferred_element_type=F32)
    return context.astype(BF).reshape(length, -1), probs, probs_b, four


def local(
    tokens, par_gain, par_wq, par_wk, par_wv, par_wo, var_wq, var_wk, var_wv, var_wo, lin_w, windows
):
    section = lax.axis_index("section")
    d = lax.axis_index("dp")
    z = lax.axis_index(Z)
    xh = lax.axis_index("xh")
    core = lax.axis_index("core")
    _, length, width = tokens.shape
    rows = par_wq.shape[1]
    cols = par_wq.shape[2]
    kv_cols = par_wk.shape[2]
    n_dp = lax.axis_size("dp")
    all_tokens = n_dp * length
    inv_scale = float(all_tokens) ** (-0.5)
    n_model = par_gain.shape[1]
    gain = lax.dynamic_slice_in_dim(par_gain[0], d * rows, rows, 0)
    positions = jnp.arange(length, dtype=jnp.int32)
    causal = positions[None, :] <= positions[:, None]
    windowed = causal & (positions[None, :] > positions[:, None] - windows[0])
    at = jnp.stack([z, core, xh, d])

    tok = tokens[0]
    tok_pair = ordered(turned(tok), turned(tok, 1), xh)

    def gained(weight):
        return (weight[0].astype(F32) * gain[:, None]).astype(BF)

    def kv_weight(weight_k, weight_v):
        own = jnp.stack([gained(weight_k).T, gained(weight_v).T])
        two = jnp.stack([own, partner(own, "xh")])
        return jnp.concatenate([two, partner(two, "core")])

    par_q = gained(par_wq)
    par_kv = kv_weight(par_wk, par_wv)
    stu_q = gained(var_wq)
    stu_kv = kv_weight(var_wk, var_wv)
    lin_in = gained(lin_w)
    stu_back = var_wo[0].T

    def scale_of(summed):
        mean = (summed[:, 0:1] + summed[:, 1:2]) / n_model
        return lax.rsqrt(mean + 1e-05)

    def cut(sums, scale, first):
        heads = (sums[:, first : first + cols + 2 * HD] * scale).astype(BF)
        return heads[:, :cols], heads[:, cols : cols + HD], heads[:, cols + HD :]

    def summed_out(contexts, weights):
        contexts = gather_dp(contexts)
        first_away, rest_away, first, rest = out_blocks(at, contexts, weights)
        first_away = partner(first_away, "core")
        rest_away = partner(rest_away, "core")
        pair = scatter_z(
            lambda i, j: first[i:j] + first_away[i:j].astype(F32),
            lambda i, j: rest[i:j] + rest_away[i:j].astype(F32),
        )
        return pair.astype(BF), contexts

    got, (par_q, par_kv) = gather_z(tok_pair, (par_q, par_kv))
    part, _, _ = gathered_dot(at, got, [par_q], [par_kv], True)
    sums = summed(scatter_dp(part))
    scale = scale_of(sums[:, cols + 2 * HD :])
    context = attend(*cut(sums, scale, 0), causal)[0]
    pair, _ = summed_out(context[None], [par_wo[0]])
    pair = pair[0]
    to_next = [
        lax.ppermute(pair, ("section", "xh"), [(h, 2 + (h ^ flip)) for h in range(2)])
        for flip in range(2)
    ]
    next_pair = tok_pair.astype(F32) + (to_next[0].astype(F32) + to_next[1].astype(F32))
    in_pair = jnp.where(section == 0, tok_pair, next_pair.astype(BF))

    got, (stu_q, stu_kv, lin_in, stu_back) = gather_z(
        in_pair, (stu_q, stu_kv, lin_in, stu_back)
    )
    part, x, (linear,) = gathered_dot(
        at, got, [par_q, stu_q], [par_kv, stu_kv], True, [lin_in]
    )
    sums = summed(scatter_dp(part))
    linear = lax.psum_scatter(linear, "dp", scatter_dimension=0, tiled=True)
    kv_first = 2 * cols
    scale = scale_of(sums[:, kv_first + 4 * HD :])
    heads = jnp.concatenate(
        [
            sums[:, :cols],
            sums[:, kv_first : kv_first + 2 * HD],
            sums[:, cols : 2 * cols],
            sums[:, kv_first + 2 * HD : kv_first + 4 * HD],
        ],
        axis=1,
    )
    par_context = attend(*cut(heads, scale, 0), causal)[0]
    queries, keys, values = cut(heads, scale, cols + 2 * HD)
    stu_context, probs, probs_b, query_four = attend(queries, keys, values, windowed)
    pair, contexts = summed_out(
        jnp.stack([par_context, stu_context]), [par_wo[0], var_wo[0]]
    )
    stu_all = jnp.concatenate([context[1] for context in contexts])
    pair = pair.astype(F32) + partner(pair, "xh").astype(F32)
    target, above = pair[0], pair[1]
    grad_student = (above * inv_scale).astype(BF)

    own_target = lax.dynamic_index_in_dim(target, xh, 0, keepdims=False)
    own_in = lax.dynamic_index_in_dim(in_pair, xh, 0, keepdims=False)
    own_out = (own_in.astype(F32) + own_target).astype(BF)
    back = turned(jnp.stack([own_out, own_target.astype(BF)]))
    layer_out = back[0]
    got, (back_target,) = gather_z(grad_student, (back[1],))
    grad_linear = linear.astype(F32) * scale - back_target.astype(F32)
    grad_linear = (grad_linear * inv_scale).astype(BF)
    grad_linear = (grad_linear.astype(F32) * scale).astype(BF)

    part, gs, _ = gathered_dot(at, got, [stu_back], [], False)
    grad_context = summed(scatter_dp(part)).astype(BF)
    grad_four = grad_context.reshape(length, -1, HD)
    grad_probs = jnp.einsum("igd,jd->gij", grad_four, values, preferred_element_type=F32)
    grad_scores = probs * (grad_probs - jnp.sum(grad_probs * probs, axis=-1, keepdims=True))
    grad_scaled = (grad_scores * HD ** (-0.5)).astype(BF)
    grad_q = jnp.einsum("gij,jd->igd", grad_scaled, keys, preferred_element_type=F32)
    grad_q = (grad_q.reshape(length, cols) * scale).astype(BF)
    grad_k = jnp.einsum("gij,igd->dj", grad_scaled, query_four, preferred_element_type=F32)
    grad_v = jnp.einsum("gij,igd->dj", probs_b, grad_four, preferred_element_type=F32)
    members = HD // kv_cols
    parts = jnp.concatenate(
        [grad_k.reshape(members, kv_cols, length), grad_v.reshape(members, kv_cols, length)], axis=1
    )
    parts = (parts * scale.reshape(1, 1, length)).reshape(2, 2, 2 * kv_cols, length)

    def reduced(blocks, axis, at_axis, along):
        kept = lax.dynamic_index_in_dim(blocks, at_axis, along, keepdims=False)
        sent = lax.dynamic_index_in_dim(blocks, 1 - at_axis, along, keepdims=False)
        return kept + partner(sent.astype(BF), axis).astype(F32)

    parts = reduced(reduced(parts, "core", core, 1), "xh", xh, 0).astype(BF)
    grads = jnp.concatenate(gather_dp(jnp.concatenate([grad_q, grad_linear], axis=1)))
    grad_q, grad_linear = grads[:, :cols], grads[:, cols:]
    grad_kv = jnp.concatenate(gather_dp(parts), axis=1)

    over_tokens = ((0,), (0,))
    column = gain[:, None]
    grad_wq = dot(x, grad_q, over_tokens) * column
    grad_wkv = dot(x, grad_kv, ((0,), (1,))) * column
    grad_wo = dot(stu_all, gs, over_tokens)
    grad_lin = dot(x, grad_linear, over_tokens) * column
    return (
        layer_out[None, None],
        grad_wq[None],
        grad_wkv[None, :, :kv_cols],
        grad_wkv[None, :, kv_cols:],
        grad_wo[None],
        grad_lin[None],
    )


def solution(mesh):
    sizes = (mesh.shape["section"], mesh.shape["dp"], 4, 2, 2, 2)
    fine = Mesh(mesh.devices.reshape(sizes), ("section", "dp") + MP)
    by_columns = P("section", "dp", MP)
    by_rows = P("section", MP, "dp")
    return jax.shard_map(
        local,
        mesh=fine,
        in_specs=(
            P("dp", None, MP),
            P("section", None),
            by_columns,
            by_columns,
            by_columns,
            by_rows,
            by_columns,
            by_columns,
            by_columns,
            by_rows,
            by_columns,
            P("section"),
        ),
        out_specs=(
            P("section", "dp", None, MP),
            by_columns,
            by_columns,
            by_columns,
            by_rows,
            by_columns,
        ),
        check_vma=False,
    )
```

```python
import functools

import jax
import jax.numpy as jnp
from jax import lax
from jax.experimental import pallas as pl
from jax.experimental.pallas import tpu as pltpu
from jax.sharding import Mesh, PartitionSpec as P

HQ = 64
KVH = 8
HD = 128
MP = ("zh", "zl", "xh", "core")
Z = ("zh", "zl")
BF = jnp.bfloat16
F32 = jnp.float32


def dot(left, right, dims):
    return lax.dot_general(left, right, (dims, ((), ())), preferred_element_type=F32)


def shift_table(count, distance):
    return [(i, (i + distance) % count) for i in range(count)]


def ordered(own, other, at):
    return jnp.where(at == 0, jnp.stack([own, other]), jnp.stack([other, own]))


def partner(block, axis):
    return lax.ppermute(block, axis, [(0, 1), (1, 0)])


def turn_table(flip):
    return [
        ((a * 4 + b) * 2 + h, (b * 4 + a) * 2 + (h ^ flip))
        for a in range(4)
        for b in range(4)
        for h in range(2)
    ]


def turned(block, flip=0):
    return lax.ppermute(block, ("dp", "zh", "xh"), turn_table(flip))


def ahead(block, hops):
    table = []
    for z in range(8):
        table.append((z * 2, (z + hops) % 8 * 2))
        table.append((z * 2 + 1, (z - hops) % 8 * 2 + 1))
    return lax.ppermute(block, Z + ("core",), table)


def gather_z(pair, beside=(), after=()):
    quad = jnp.stack([pair, partner(pair, "core")])
    one = ahead(quad, 1)
    two = ahead(quad, 2)
    if beside:
        two, *beside = lax.optimization_barrier((two, *beside))
    three = ahead(two, 1)
    four = ahead(two[0], 2)
    if after:
        three, four, *after = lax.optimization_barrier((three, four, *after))
    mine = [one, two, three, four]
    theirs = [partner(block, "core") for block in mine]
    return (quad, mine, theirs), beside, after


def scatter_z(first, rest):
    next_two = jnp.concatenate([first(0, 2), rest(0, 2)]).astype(BF)
    s4 = first(2, 3)[0].astype(BF)
    hop = ahead(next_two, 1)
    four = ahead(s4, 2)
    three, one = hop[:2], hop[2:]
    s2 = rest(2, 4) + three.astype(F32)
    s2 = jnp.stack([s2[0] + four.astype(F32), s2[1]]).astype(BF)
    two = ahead(s2, 2)
    total = one.astype(F32) + two.astype(F32)
    across = partner(total[1].astype(BF), "core")
    return rest(4, 5)[0] + total[0] + across.astype(F32)


def scatter_dp(blocks):
    got = [lax.ppermute(blocks[k], "dp", shift_table(4, k)) for k in (2, 1, 3)]
    return [blocks[0]] + got


def summed(blocks):
    total = blocks[0].astype(F32)
    for block in blocks[1:]:
        total = total + block.astype(F32)
    return total


def gather_dp(block):
    got = {k: lax.ppermute(block, "dp", shift_table(4, 4 - k)) for k in (2, 1, 3)}
    return [block, got[1], got[2], got[3]]


def in_kernel(counts, squares, at, quad, *refs):
    mine, theirs, refs = refs[:4], refs[4:8], refs[8:]
    weights, refs = refs[: counts[0]], refs[counts[0] :]
    sides, refs = refs[: counts[1]], refs[counts[1] :]
    kvs, refs = refs[: counts[2]], refs[counts[2] :]
    outs, x, asides, kv_rows = refs[:4], refs[4], refs[5:-1], refs[-1]
    length, width = quad.shape[2], quad.shape[3]
    z0, core, xh, d = at[0], at[1], at[2], at[3]
    up = 2 * core - 1

    def place(block, z, feature_core):
        z = (z + 8) & 7
        first = pl.multiple_of((((z >> 1) - d) & 3) * length, length)
        for h in range(2):
            column = pl.multiple_of((((z & 1) * 2 + h) * 2 + feature_core) * width, width)
            x[pl.ds(first, length), pl.ds(column, width)] = block[h]

    for i in range(2):
        place(quad.at[i], z0, core ^ i)
    for hops in range(1, 4):
        for i in range(2):
            place(mine[hops - 1].at[i], z0 + up * hops, core ^ i)
            place(theirs[hops - 1].at[i], z0 - up * hops, core ^ i ^ 1)
    place(mine[3], z0 + 4, core)
    place(theirs[3], z0 + 4, core ^ 1)

    column = 0

    def put(product):
        for k in range(4):
            outs[k][:, column : column + product.shape[1]] = product[
                k * length : (k + 1) * length
            ].astype(BF)

    for weight in weights:
        put(jnp.dot(x[...], weight[...], preferred_element_type=F32))
        column += weight.shape[1]
    for kv in kvs:
        rows = kv.shape[2]
        for slot in range(4):
            member = ((slot & 1) ^ xh) * 2 + ((slot >> 1) ^ core)
            first = pl.multiple_of(member * rows, rows)
            for which in range(2):
                kv_rows[pl.ds(first + which * 4 * rows, rows), :] = kv[slot, which]
        put(
            lax.dot_general(
                x[...], kv_rows[...], (((1,), (1,)), ((), ())), preferred_element_type=F32
            )
        )
        column += 8 * rows
    if squares:
        for k in range(4):
            total = jnp.zeros((length, HD), F32)
            for lane in range(0, x.shape[1], HD):
                wide = x[k * length : (k + 1) * length, lane : lane + HD].astype(F32)
                total = total + wide * wide
            sums = jnp.sum(total, axis=1, keepdims=True)
            high = sums.astype(BF).astype(F32)
            lane = lax.broadcasted_iota(jnp.int32, (length, HD), 1)
            both = jnp.where(lane == 0, high, jnp.where(lane == 1, sums - high, 0.0))
            outs[k][:, column:] = both.astype(BF)
    for weight, aside in zip(sides, asides):
        product = jnp.dot(x[...], weight[...], preferred_element_type=F32).astype(BF)
        for k in range(4):
            first = pl.multiple_of(((k + d) & 3) * length, length)
            aside[pl.ds(first, length), :] = product[k * length : (k + 1) * length]


def gathered_dot(at, gathered, weights, kvs, squares, sides=()):
    quad, mine, theirs = gathered
    length, width = quad.shape[2:]
    depth = weights[0].shape[0]
    tokens = 4 * length
    columns = sum(w.shape[1] for w in weights) + sum(8 * kv.shape[2] for kv in kvs)
    wide = columns + (HD if squares else 0)
    kv_shape = (2 * HD, depth) if kvs else (16, HD)
    vmem = pl.BlockSpec(memory_space=pltpu.VMEM)
    operands = [quad, *mine, *theirs, *weights, *sides, *kvs]
    shapes = [(length, wide)] * 4 + [(tokens, depth)] + [(tokens, w.shape[1]) for w in sides]
    out = pl.pallas_call(
        functools.partial(in_kernel, (len(weights), len(sides), len(kvs)), squares),
        out_shape=tuple(jax.ShapeDtypeStruct(shape, BF) for shape in shapes),
        in_specs=[pl.BlockSpec(memory_space=pltpu.SMEM)] + [vmem] * len(operands),
        out_specs=(vmem,) * len(shapes),
        scratch_shapes=[pltpu.VMEM(kv_shape, BF)],
        compiler_params=pltpu.CompilerParams(vmem_limit_bytes=32 << 20),
        cost_estimate=pl.CostEstimate(
            flops=2 * tokens * depth * columns,
            bytes_accessed=2 * depth * (columns + 2 * tokens),
            transcendentals=0,
        ),
    )(at, *operands)
    return out[:4], out[4], out[5:]


FIRST = ((3, 0), (3, 1), (4, 0))
REST = ((1, 0), (1, 1), (2, 0), (2, 1), (0, 0))


def out_kernel(count, at, *refs):
    contexts, weights = refs[:4], refs[4 : 4 + count]
    outs, rows = refs[4 + count : 8 + count], refs[8 + count]
    length, width = outs[0].shape[3:]
    z0, own_core, d = at[0], at[1], at[3]
    for k in range(4):
        rows[k] = contexts[k][...]
    for out, units, core in (
        (outs[0], FIRST, 1 - own_core),
        (outs[1], REST, 1 - own_core),
        (outs[2], FIRST, own_core),
        (outs[3], REST, own_core),
    ):
        for unit, (hops, other) in enumerate(units):
            z = (z0 + (1 - 2 * core) * hops + 8) & 7
            k = ((z >> 1) - d) & 3
            for h in range(2):
                column = (((z & 1) * 2 + h) * 2 + (core ^ other)) * width
                column = pl.multiple_of(column, width)
                terms = [
                    jnp.dot(
                        rows[k, i], weight[:, pl.ds(column, width)], preferred_element_type=F32
                    )
                    for i, weight in enumerate(weights)
                ]
                if count == 2:
                    terms[1] = terms[1] - terms[0]
                for i, term in enumerate(terms):
                    out[unit, i, h] = term.astype(out.dtype)


def out_blocks(at, contexts, weights):
    count, length, cols = contexts[0].shape
    depth = weights[0].shape[1]
    width = depth // 8
    vmem = pl.BlockSpec(memory_space=pltpu.VMEM)
    unit = (count, 2, length, width)
    return pl.pallas_call(
        functools.partial(out_kernel, count),
        out_shape=tuple(
            jax.ShapeDtypeStruct((len(units),) + unit, kind)
            for kind in (BF, F32)
            for units in (FIRST, REST)
        ),
        in_specs=[pl.BlockSpec(memory_space=pltpu.SMEM)] + [vmem] * (4 + count),
        out_specs=(vmem,) * 4,
        scratch_shapes=[pltpu.VMEM((4, count, length, cols), BF)],
        compiler_params=pltpu.CompilerParams(vmem_limit_bytes=24 << 20),
        cost_estimate=pl.CostEstimate(
            flops=8 * count * length * cols * depth,
            bytes_accessed=count * (2 * cols * depth + 24 * length * depth),
            transcendentals=0,
        ),
    )(at, *contexts, *weights)


def attend(queries, keys, values, keep):
    length = queries.shape[0]
    four = queries.reshape(length, -1, HD)
    scores = jnp.einsum("igd,jd->gij", four, keys, preferred_element_type=F32) * HD ** (-0.5)
    probs = jax.nn.softmax(jnp.where(keep, scores, -1e30), axis=-1)
    probs_b = probs.astype(BF)
    context = jnp.einsum("gij,jd->igd", probs_b, values, preferred_element_type=F32)
    return context.astype(BF).reshape(length, -1), probs, probs_b, four


def local(
    tokens, par_gain, par_wq, par_wk, par_wv, par_wo, var_wq, var_wk, var_wv, var_wo, lin_w, windows
):
    section = lax.axis_index("section")
    d = lax.axis_index("dp")
    z = lax.axis_index(Z)
    xh = lax.axis_index("xh")
    core = lax.axis_index("core")
    _, length, width = tokens.shape
    rows = par_wq.shape[1]
    cols = par_wq.shape[2]
    kv_cols = par_wk.shape[2]
    n_dp = lax.axis_size("dp")
    all_tokens = n_dp * length
    inv_scale = float(all_tokens) ** (-0.5)
    n_model = par_gain.shape[1]
    gain = lax.dynamic_slice_in_dim(par_gain[0], d * rows, rows, 0)
    positions = jnp.arange(length, dtype=jnp.int32)
    causal = positions[None, :] <= positions[:, None]
    windowed = causal & (positions[None, :] > positions[:, None] - windows[0])
    at = jnp.stack([z, core, xh, d])

    tok = tokens[0]
    tok_pair = ordered(turned(tok), turned(tok, 1), xh)

    def gained(weight):
        return (weight[0].astype(F32) * gain[:, None]).astype(BF)

    def kv_weight(weight_k, weight_v):
        own = jnp.stack([gained(weight_k).T, gained(weight_v).T])
        two = jnp.stack([own, partner(own, "xh")])
        return jnp.concatenate([two, partner(two, "core")])

    par_q = gained(par_wq)
    par_kv = kv_weight(par_wk, par_wv)
    stu_q = gained(var_wq)
    stu_kv = kv_weight(var_wk, var_wv)
    lin_in = gained(lin_w)
    stu_back = var_wo[0].T

    def scale_of(summed):
        mean = (summed[:, 0:1] + summed[:, 1:2]) / n_model
        return lax.rsqrt(mean + 1e-05)

    def cut(sums, scale, first):
        heads = (sums[:, first : first + cols + 2 * HD] * scale).astype(BF)
        return heads[:, :cols], heads[:, cols : cols + HD], heads[:, cols + HD :]

    def summed_out(contexts, weights, beside=()):
        contexts = gather_dp(contexts)
        if beside:
            *contexts, beside = lax.optimization_barrier((*contexts, beside))
        first_away, rest_away, first, rest = out_blocks(at, contexts, weights)
        first_away = partner(first_away, "core")
        rest_away = partner(rest_away, "core")
        pair = scatter_z(
            lambda i, j: first[i:j] + first_away[i:j].astype(F32),
            lambda i, j: rest[i:j] + rest_away[i:j].astype(F32),
        )
        return pair.astype(BF), contexts, beside

    got, (par_q, par_kv), _ = gather_z(tok_pair, (par_q, par_kv))
    part, _, _ = gathered_dot(at, got, [par_q], [par_kv], True)
    sums = summed(scatter_dp(part))
    scale = scale_of(sums[:, cols + 2 * HD :])
    context = attend(*cut(sums, scale, 0), causal)[0]
    pair, _, (stu_q, stu_kv, lin_in, stu_back) = summed_out(
        context[None], [par_wo[0]], (stu_q, stu_kv, lin_in, stu_back)
    )
    pair = pair[0]
    to_next = [
        lax.ppermute(pair, ("section", "xh"), [(h, 2 + (h ^ flip)) for h in range(2)])
        for flip in range(2)
    ]
    next_pair = tok_pair.astype(F32) + (to_next[0].astype(F32) + to_next[1].astype(F32))
    in_pair = jnp.where(section == 0, tok_pair, next_pair.astype(BF))

    got, _, _ = gather_z(in_pair)
    part, x, (linear,) = gathered_dot(
        at, got, [par_q, stu_q], [par_kv, stu_kv], True, [lin_in]
    )
    sums = summed(scatter_dp(part))
    linear = lax.psum_scatter(linear, "dp", scatter_dimension=0, tiled=True)
    kv_first = 2 * cols
    scale = scale_of(sums[:, kv_first + 4 * HD :])
    heads = jnp.concatenate(
        [
            sums[:, :cols],
            sums[:, kv_first : kv_first + 2 * HD],
            sums[:, cols : 2 * cols],
            sums[:, kv_first + 2 * HD : kv_first + 4 * HD],
        ],
        axis=1,
    )
    par_context = attend(*cut(heads, scale, 0), causal)[0]
    queries, keys, values = cut(heads, scale, cols + 2 * HD)
    stu_context, probs, probs_b, query_four = attend(queries, keys, values, windowed)
    pair, contexts, _ = summed_out(
        jnp.stack([par_context, stu_context]), [par_wo[0], var_wo[0]]
    )
    stu_all = jnp.concatenate([context[1] for context in contexts])
    pair = pair.astype(F32) + partner(pair, "xh").astype(F32)
    target, above = pair[0], pair[1]
    grad_student = (above * inv_scale).astype(BF)

    own_target = lax.dynamic_index_in_dim(target, xh, 0, keepdims=False)
    own_in = lax.dynamic_index_in_dim(in_pair, xh, 0, keepdims=False)
    own_out = (own_in.astype(F32) + own_target).astype(BF)
    back = jnp.stack([own_out, own_target.astype(BF)])
    got, _, (back,) = gather_z(grad_student, (), (back,))
    back = turned(back)
    layer_out = back[0]
    grad_linear = linear.astype(F32) * scale - back[1].astype(F32)
    grad_linear = (grad_linear * inv_scale).astype(BF)
    grad_linear = (grad_linear.astype(F32) * scale).astype(BF)

    part, gs, _ = gathered_dot(at, got, [stu_back], [], False)
    grad_context = summed(scatter_dp(part)).astype(BF)
    grad_four = grad_context.reshape(length, -1, HD)
    grad_probs = jnp.einsum("igd,jd->gij", grad_four, values, preferred_element_type=F32)
    grad_scores = probs * (grad_probs - jnp.sum(grad_probs * probs, axis=-1, keepdims=True))
    grad_scaled = (grad_scores * HD ** (-0.5)).astype(BF)
    grad_q = jnp.einsum("gij,jd->igd", grad_scaled, keys, preferred_element_type=F32)
    grad_q = (grad_q.reshape(length, cols) * scale).astype(BF)
    grad_k = jnp.einsum("gij,igd->dj", grad_scaled, query_four, preferred_element_type=F32)
    grad_v = jnp.einsum("gij,igd->dj", probs_b, grad_four, preferred_element_type=F32)
    members = HD // kv_cols
    parts = jnp.concatenate(
        [grad_k.reshape(members, kv_cols, length), grad_v.reshape(members, kv_cols, length)], axis=1
    )
    parts = (parts * scale.reshape(1, 1, length)).reshape(2, 2, 2 * kv_cols, length)

    def reduced(blocks, axis, at_axis, along):
        kept = lax.dynamic_index_in_dim(blocks, at_axis, along, keepdims=False)
        sent = lax.dynamic_index_in_dim(blocks, 1 - at_axis, along, keepdims=False)
        return kept + partner(sent.astype(BF), axis).astype(F32)

    parts = reduced(reduced(parts, "core", core, 1), "xh", xh, 0).astype(BF)
    grads = jnp.concatenate(gather_dp(jnp.concatenate([grad_q, grad_linear], axis=1)))
    grads, parts = lax.optimization_barrier((grads, parts))
    grad_q, grad_linear = grads[:, :cols], grads[:, cols:]
    grad_kv = jnp.concatenate(gather_dp(parts), axis=1)

    over_tokens = ((0,), (0,))
    column = gain[:, None]
    grad_wq = dot(x, grad_q, over_tokens) * column
    grad_wkv = dot(x, grad_kv, ((0,), (1,))) * column
    grad_wo = dot(stu_all, gs, over_tokens)
    grad_lin = dot(x, grad_linear, over_tokens) * column
    return (
        layer_out[None, None],
        grad_wq[None],
        grad_wkv[None, :, :kv_cols],
        grad_wkv[None, :, kv_cols:],
        grad_wo[None],
        grad_lin[None],
    )


def solution(mesh):
    sizes = (mesh.shape["section"], mesh.shape["dp"], 4, 2, 2, 2)
    fine = Mesh(mesh.devices.reshape(sizes), ("section", "dp") + MP)
    by_columns = P("section", "dp", MP)
    by_rows = P("section", MP, "dp")
    return jax.shard_map(
        local,
        mesh=fine,
        in_specs=(
            P("dp", None, MP),
            P("section", None),
            by_columns,
            by_columns,
            by_columns,
            by_rows,
            by_columns,
            by_columns,
            by_columns,
            by_rows,
            by_columns,
            P("section"),
        ),
        out_specs=(
            P("section", "dp", None, MP),
            by_columns,
            by_columns,
            by_columns,
            by_rows,
            by_columns,
        ),
        check_vma=False,
    )
```

```python
import functools

import jax
import jax.numpy as jnp
from jax import lax
from jax.experimental import pallas as pl
from jax.experimental.pallas import tpu as pltpu
from jax.sharding import Mesh, PartitionSpec as P

HQ = 64
KVH = 8
HD = 128
MP = ("zh", "zl", "xh", "core")
Z = ("zh", "zl")
BF = jnp.bfloat16
F32 = jnp.float32


def dot(left, right, dims):
    return lax.dot_general(left, right, (dims, ((), ())), preferred_element_type=F32)


def shift_table(count, distance):
    return [(i, (i + distance) % count) for i in range(count)]


def ordered(own, other, at):
    return jnp.where(at == 0, jnp.stack([own, other]), jnp.stack([other, own]))


def partner(block, axis):
    return lax.ppermute(block, axis, [(0, 1), (1, 0)])


def turn_table(flip):
    return [
        ((a * 4 + b) * 2 + h, (b * 4 + a) * 2 + (h ^ flip))
        for a in range(4)
        for b in range(4)
        for h in range(2)
    ]


def turned(block, flip=0):
    return lax.ppermute(block, ("dp", "zh", "xh"), turn_table(flip))


def ahead(block, hops):
    table = []
    for z in range(8):
        table.append((z * 2, (z + hops) % 8 * 2))
        table.append((z * 2 + 1, (z - hops) % 8 * 2 + 1))
    return lax.ppermute(block, Z + ("core",), table)


def gather_z(pair, beside=(), after=()):
    quad = jnp.stack([pair, partner(pair, "core")])
    one = ahead(quad, 1)
    two = ahead(quad, 2)
    if beside:
        two, *beside = lax.optimization_barrier((two, *beside))
    if after:
        two, *after = lax.optimization_barrier((two, *after))
    three = ahead(two, 1)
    four = ahead(two[0], 2)
    mine = [one, two, three, four]
    theirs = [partner(block, "core") for block in mine]
    return (quad, mine, theirs), beside, after


def scatter_z(first, rest, beside=()):
    next_two = jnp.concatenate([first(0, 2), rest(0, 2)]).astype(BF)
    s4 = first(2, 3)[0].astype(BF)
    hop = ahead(next_two, 1)
    four = ahead(s4, 2)
    if beside:
        hop, *beside = lax.optimization_barrier((hop, *beside))
    three, one = hop[:2], hop[2:]
    s2 = rest(2, 4) + three.astype(F32)
    s2 = jnp.stack([s2[0] + four.astype(F32), s2[1]]).astype(BF)
    two = ahead(s2, 2)
    total = one.astype(F32) + two.astype(F32)
    across = partner(total[1].astype(BF), "core")
    return rest(4, 5)[0] + total[0] + across.astype(F32), beside


def scatter_dp(blocks):
    got = [lax.ppermute(blocks[k], "dp", shift_table(4, k)) for k in (2, 1, 3)]
    return [blocks[0]] + got


def summed(blocks):
    total = blocks[0].astype(F32)
    for block in blocks[1:]:
        total = total + block.astype(F32)
    return total


def gather_dp(block):
    got = {k: lax.ppermute(block, "dp", shift_table(4, 4 - k)) for k in (2, 1, 3)}
    return [block, got[1], got[2], got[3]]


def in_kernel(counts, squares, at, quad, *refs):
    mine, theirs, refs = refs[:4], refs[4:8], refs[8:]
    weights, refs = refs[: counts[0]], refs[counts[0] :]
    sides, refs = refs[: counts[1]], refs[counts[1] :]
    kvs, refs = refs[: counts[2]], refs[counts[2] :]
    outs, x, asides, kv_rows = refs[:4], refs[4], refs[5:-1], refs[-1]
    length, width = quad.shape[2], quad.shape[3]
    z0, core, xh, d = at[0], at[1], at[2], at[3]
    up = 2 * core - 1

    def place(block, z, feature_core):
        z = (z + 8) & 7
        first = pl.multiple_of((((z >> 1) - d) & 3) * length, length)
        for h in range(2):
            column = pl.multiple_of((((z & 1) * 2 + h) * 2 + feature_core) * width, width)
            x[pl.ds(first, length), pl.ds(column, width)] = block[h]

    for i in range(2):
        place(quad.at[i], z0, core ^ i)
    for hops in range(1, 4):
        for i in range(2):
            place(mine[hops - 1].at[i], z0 + up * hops, core ^ i)
            place(theirs[hops - 1].at[i], z0 - up * hops, core ^ i ^ 1)
    place(mine[3], z0 + 4, core)
    place(theirs[3], z0 + 4, core ^ 1)

    column = 0

    def put(product):
        for k in range(4):
            outs[k][:, column : column + product.shape[1]] = product[
                k * length : (k + 1) * length
            ].astype(BF)

    for weight in weights:
        put(jnp.dot(x[...], weight[...], preferred_element_type=F32))
        column += weight.shape[1]
    for kv in kvs:
        rows = kv.shape[2]
        for slot in range(4):
            member = ((slot & 1) ^ xh) * 2 + ((slot >> 1) ^ core)
            first = pl.multiple_of(member * rows, rows)
            for which in range(2):
                kv_rows[pl.ds(first + which * 4 * rows, rows), :] = kv[slot, which]
        put(
            lax.dot_general(
                x[...], kv_rows[...], (((1,), (1,)), ((), ())), preferred_element_type=F32
            )
        )
        column += 8 * rows
    if squares:
        for k in range(4):
            total = jnp.zeros((length, HD), F32)
            for lane in range(0, x.shape[1], HD):
                wide = x[k * length : (k + 1) * length, lane : lane + HD].astype(F32)
                total = total + wide * wide
            sums = jnp.sum(total, axis=1, keepdims=True)
            high = sums.astype(BF).astype(F32)
            lane = lax.broadcasted_iota(jnp.int32, (length, HD), 1)
            both = jnp.where(lane == 0, high, jnp.where(lane == 1, sums - high, 0.0))
            outs[k][:, column:] = both.astype(BF)
    for weight, aside in zip(sides, asides):
        product = jnp.dot(x[...], weight[...], preferred_element_type=F32).astype(BF)
        for k in range(4):
            first = pl.multiple_of(((k + d) & 3) * length, length)
            aside[pl.ds(first, length), :] = product[k * length : (k + 1) * length]


def gathered_dot(at, gathered, weights, kvs, squares, sides=()):
    quad, mine, theirs = gathered
    length, width = quad.shape[2:]
    depth = weights[0].shape[0]
    tokens = 4 * length
    columns = sum(w.shape[1] for w in weights) + sum(8 * kv.shape[2] for kv in kvs)
    wide = columns + (HD if squares else 0)
    kv_shape = (2 * HD, depth) if kvs else (16, HD)
    vmem = pl.BlockSpec(memory_space=pltpu.VMEM)
    operands = [quad, *mine, *theirs, *weights, *sides, *kvs]
    shapes = [(length, wide)] * 4 + [(tokens, depth)] + [(tokens, w.shape[1]) for w in sides]
    out = pl.pallas_call(
        functools.partial(in_kernel, (len(weights), len(sides), len(kvs)), squares),
        out_shape=tuple(jax.ShapeDtypeStruct(shape, BF) for shape in shapes),
        in_specs=[pl.BlockSpec(memory_space=pltpu.SMEM)] + [vmem] * len(operands),
        out_specs=(vmem,) * len(shapes),
        scratch_shapes=[pltpu.VMEM(kv_shape, BF)],
        compiler_params=pltpu.CompilerParams(vmem_limit_bytes=32 << 20),
        cost_estimate=pl.CostEstimate(
            flops=2 * tokens * depth * columns,
            bytes_accessed=2 * depth * (columns + 2 * tokens),
            transcendentals=0,
        ),
    )(at, *operands)
    return out[:4], out[4], out[5:]


FIRST = ((3, 0), (3, 1), (4, 0))
REST = ((1, 0), (1, 1), (2, 0), (2, 1), (0, 0))


def out_kernel(count, at, *refs):
    contexts, weights = refs[:4], refs[4 : 4 + count]
    outs, rows = refs[4 + count : 8 + count], refs[8 + count]
    length, width = outs[0].shape[3:]
    z0, own_core, d = at[0], at[1], at[3]
    for k in range(4):
        rows[k] = contexts[k][...]
    for out, units, core in (
        (outs[0], FIRST, 1 - own_core),
        (outs[1], REST, 1 - own_core),
        (outs[2], FIRST, own_core),
        (outs[3], REST, own_core),
    ):
        for unit, (hops, other) in enumerate(units):
            z = (z0 + (1 - 2 * core) * hops + 8) & 7
            k = ((z >> 1) - d) & 3
            for h in range(2):
                column = (((z & 1) * 2 + h) * 2 + (core ^ other)) * width
                column = pl.multiple_of(column, width)
                terms = [
                    jnp.dot(
                        rows[k, i], weight[:, pl.ds(column, width)], preferred_element_type=F32
                    )
                    for i, weight in enumerate(weights)
                ]
                if count == 2:
                    terms[1] = terms[1] - terms[0]
                for i, term in enumerate(terms):
                    out[unit, i, h] = term.astype(out.dtype)


def out_blocks(at, contexts, weights):
    count, length, cols = contexts[0].shape
    depth = weights[0].shape[1]
    width = depth // 8
    vmem = pl.BlockSpec(memory_space=pltpu.VMEM)
    unit = (count, 2, length, width)
    return pl.pallas_call(
        functools.partial(out_kernel, count),
        out_shape=tuple(
            jax.ShapeDtypeStruct((len(units),) + unit, kind)
            for kind in (BF, F32)
            for units in (FIRST, REST)
        ),
        in_specs=[pl.BlockSpec(memory_space=pltpu.SMEM)] + [vmem] * (4 + count),
        out_specs=(vmem,) * 4,
        scratch_shapes=[pltpu.VMEM((4, count, length, cols), BF)],
        compiler_params=pltpu.CompilerParams(vmem_limit_bytes=24 << 20),
        cost_estimate=pl.CostEstimate(
            flops=8 * count * length * cols * depth,
            bytes_accessed=count * (2 * cols * depth + 24 * length * depth),
            transcendentals=0,
        ),
    )(at, *contexts, *weights)


def attend(queries, keys, values, keep):
    length = queries.shape[0]
    four = queries.reshape(length, -1, HD)
    scores = jnp.einsum("igd,jd->gij", four, keys, preferred_element_type=F32) * HD ** (-0.5)
    probs = jax.nn.softmax(jnp.where(keep, scores, -1e30), axis=-1)
    probs_b = probs.astype(BF)
    context = jnp.einsum("gij,jd->igd", probs_b, values, preferred_element_type=F32)
    return context.astype(BF).reshape(length, -1), probs, probs_b, four


def local(
    tokens, par_gain, par_wq, par_wk, par_wv, par_wo, var_wq, var_wk, var_wv, var_wo, lin_w, windows
):
    section = lax.axis_index("section")
    d = lax.axis_index("dp")
    z = lax.axis_index(Z)
    xh = lax.axis_index("xh")
    core = lax.axis_index("core")
    _, length, width = tokens.shape
    rows = par_wq.shape[1]
    cols = par_wq.shape[2]
    kv_cols = par_wk.shape[2]
    n_dp = lax.axis_size("dp")
    all_tokens = n_dp * length
    inv_scale = float(all_tokens) ** (-0.5)
    n_model = par_gain.shape[1]
    gain = lax.dynamic_slice_in_dim(par_gain[0], d * rows, rows, 0)
    positions = jnp.arange(length, dtype=jnp.int32)
    causal = positions[None, :] <= positions[:, None]
    windowed = causal & (positions[None, :] > positions[:, None] - windows[0])
    at = jnp.stack([z, core, xh, d])

    tok = tokens[0]
    tok_pair = ordered(turned(tok), turned(tok, 1), xh)

    def gained(weight):
        return (weight[0].astype(F32) * gain[:, None]).astype(BF)

    def kv_weight(weight_k, weight_v):
        own = jnp.stack([gained(weight_k).T, gained(weight_v).T])
        two = jnp.stack([own, partner(own, "xh")])
        return jnp.concatenate([two, partner(two, "core")])

    par_q = gained(par_wq)
    par_kv = kv_weight(par_wk, par_wv)
    stu_q = gained(var_wq)
    stu_kv = kv_weight(var_wk, var_wv)
    lin_in = gained(lin_w)
    stu_back = var_wo[0].T

    def scale_of(summed):
        mean = (summed[:, 0:1] + summed[:, 1:2]) / n_model
        return lax.rsqrt(mean + 1e-05)

    def cut(sums, scale, first):
        heads = (sums[:, first : first + cols + 2 * HD] * scale).astype(BF)
        return heads[:, :cols], heads[:, cols : cols + HD], heads[:, cols + HD :]

    def summed_out(contexts, weights, beside=()):
        contexts = gather_dp(contexts)
        first_away, rest_away, first, rest = out_blocks(at, contexts, weights)
        first_away = partner(first_away, "core")
        rest_away = partner(rest_away, "core")
        pair, beside = scatter_z(
            lambda i, j: first[i:j] + first_away[i:j].astype(F32),
            lambda i, j: rest[i:j] + rest_away[i:j].astype(F32),
            beside,
        )
        return pair.astype(BF), contexts, beside

    got, (par_q, par_kv), _ = gather_z(tok_pair, (par_q, par_kv))
    part, _, _ = gathered_dot(at, got, [par_q], [par_kv], True)
    sums = summed(scatter_dp(part))
    scale = scale_of(sums[:, cols + 2 * HD :])
    context = attend(*cut(sums, scale, 0), causal)[0]
    pair, _, (stu_q, stu_kv, lin_in, stu_back) = summed_out(
        context[None], [par_wo[0]], (stu_q, stu_kv, lin_in, stu_back)
    )
    pair = pair[0]
    to_next = [
        lax.ppermute(pair, ("section", "xh"), [(h, 2 + (h ^ flip)) for h in range(2)])
        for flip in range(2)
    ]
    next_pair = tok_pair.astype(F32) + (to_next[0].astype(F32) + to_next[1].astype(F32))
    in_pair = jnp.where(section == 0, tok_pair, next_pair.astype(BF))

    got, _, _ = gather_z(in_pair)
    part, x, (linear,) = gathered_dot(
        at, got, [par_q, stu_q], [par_kv, stu_kv], True, [lin_in]
    )
    sums = summed(scatter_dp(part))
    linear = lax.psum_scatter(linear, "dp", scatter_dimension=0, tiled=True)
    kv_first = 2 * cols
    scale = scale_of(sums[:, kv_first + 4 * HD :])
    heads = jnp.concatenate(
        [
            sums[:, :cols],
            sums[:, kv_first : kv_first + 2 * HD],
            sums[:, cols : 2 * cols],
            sums[:, kv_first + 2 * HD : kv_first + 4 * HD],
        ],
        axis=1,
    )
    par_context = attend(*cut(heads, scale, 0), causal)[0]
    queries, keys, values = cut(heads, scale, cols + 2 * HD)
    stu_context, probs, probs_b, query_four = attend(queries, keys, values, windowed)
    pair, contexts, _ = summed_out(
        jnp.stack([par_context, stu_context]), [par_wo[0], var_wo[0]]
    )
    stu_all = jnp.concatenate([context[1] for context in contexts])
    pair = pair.astype(F32) + partner(pair, "xh").astype(F32)
    target, above = pair[0], pair[1]
    grad_student = (above * inv_scale).astype(BF)

    own_target = lax.dynamic_index_in_dim(target, xh, 0, keepdims=False)
    own_in = lax.dynamic_index_in_dim(in_pair, xh, 0, keepdims=False)
    own_out = (own_in.astype(F32) + own_target).astype(BF)
    got, _, (own_target,) = gather_z(grad_student, (), (own_target.astype(BF),))
    grad_linear = linear.astype(F32) * scale - turned(own_target).astype(F32)
    grad_linear = (grad_linear * inv_scale).astype(BF)
    grad_linear = (grad_linear.astype(F32) * scale).astype(BF)

    part, gs, _ = gathered_dot(at, got, [stu_back], [], False)
    grad_context = summed(scatter_dp(part)).astype(BF)
    grad_four = grad_context.reshape(length, -1, HD)
    grad_probs = jnp.einsum("igd,jd->gij", grad_four, values, preferred_element_type=F32)
    grad_scores = probs * (grad_probs - jnp.sum(grad_probs * probs, axis=-1, keepdims=True))
    grad_scaled = (grad_scores * HD ** (-0.5)).astype(BF)
    grad_q = jnp.einsum("gij,jd->igd", grad_scaled, keys, preferred_element_type=F32)
    grad_q = (grad_q.reshape(length, cols) * scale).astype(BF)
    grad_k = jnp.einsum("gij,igd->dj", grad_scaled, query_four, preferred_element_type=F32)
    grad_v = jnp.einsum("gij,igd->dj", probs_b, grad_four, preferred_element_type=F32)
    members = HD // kv_cols
    parts = jnp.concatenate(
        [grad_k.reshape(members, kv_cols, length), grad_v.reshape(members, kv_cols, length)], axis=1
    )
    parts = (parts * scale.reshape(1, 1, length)).reshape(2, 2, 2 * kv_cols, length)

    def reduced(blocks, axis, at_axis, along):
        kept = lax.dynamic_index_in_dim(blocks, at_axis, along, keepdims=False)
        sent = lax.dynamic_index_in_dim(blocks, 1 - at_axis, along, keepdims=False)
        return kept + partner(sent.astype(BF), axis).astype(F32)

    parts = reduced(reduced(parts, "core", core, 1), "xh", xh, 0).astype(BF)
    grads = jnp.concatenate(gather_dp(jnp.concatenate([grad_q, grad_linear], axis=1)))
    grads, parts, own_out = lax.optimization_barrier((grads, parts, own_out))
    layer_out = turned(own_out)
    grad_q, grad_linear = grads[:, :cols], grads[:, cols:]
    grad_kv = jnp.concatenate(gather_dp(parts), axis=1)

    over_tokens = ((0,), (0,))
    column = gain[:, None]
    grad_wq = dot(x, grad_q, over_tokens) * column
    grad_wkv = dot(x, grad_kv, ((0,), (1,))) * column
    grad_wo = dot(stu_all, gs, over_tokens)
    grad_lin = dot(x, grad_linear, over_tokens) * column
    return (
        layer_out[None, None],
        grad_wq[None],
        grad_wkv[None, :, :kv_cols],
        grad_wkv[None, :, kv_cols:],
        grad_wo[None],
        grad_lin[None],
    )


def solution(mesh):
    sizes = (mesh.shape["section"], mesh.shape["dp"], 4, 2, 2, 2)
    fine = Mesh(mesh.devices.reshape(sizes), ("section", "dp") + MP)
    by_columns = P("section", "dp", MP)
    by_rows = P("section", MP, "dp")
    return jax.shard_map(
        local,
        mesh=fine,
        in_specs=(
            P("dp", None, MP),
            P("section", None),
            by_columns,
            by_columns,
            by_columns,
            by_rows,
            by_columns,
            by_columns,
            by_columns,
            by_rows,
            by_columns,
            P("section"),
        ),
        out_specs=(
            P("section", "dp", None, MP),
            by_columns,
            by_columns,
            by_columns,
            by_rows,
            by_columns,
        ),
        check_vma=False,
    )
```

```python
import functools

import jax
import jax.numpy as jnp
from jax import lax
from jax.experimental import pallas as pl
from jax.experimental.pallas import tpu as pltpu
from jax.sharding import Mesh, PartitionSpec as P

HQ = 64
KVH = 8
HD = 128
MP = ("zh", "zl", "xh", "core")
Z = ("zh", "zl")
BF = jnp.bfloat16
F32 = jnp.float32


def dot(left, right, dims):
    return lax.dot_general(left, right, (dims, ((), ())), preferred_element_type=F32)


def shift_table(count, distance):
    return [(i, (i + distance) % count) for i in range(count)]


def ordered(own, other, at):
    return jnp.where(at == 0, jnp.stack([own, other]), jnp.stack([other, own]))


def partner(block, axis):
    return lax.ppermute(block, axis, [(0, 1), (1, 0)])


def turn_table(flip):
    return [
        ((a * 4 + b) * 2 + h, (b * 4 + (a + b) % 4) * 2 + (h ^ flip))
        for a in range(4)
        for b in range(4)
        for h in range(2)
    ]


def turned(block, flip=0):
    return lax.ppermute(block, ("dp", "zh", "xh"), turn_table(flip))


def turned_back(block):
    table = [(there, here) for here, there in turn_table(0)]
    return lax.ppermute(block, ("dp", "zh", "xh"), table)


def ahead(block, hops):
    table = []
    for z in range(8):
        table.append((z * 2, (z + hops) % 8 * 2))
        table.append((z * 2 + 1, (z - hops) % 8 * 2 + 1))
    return lax.ppermute(block, Z + ("core",), table)


def gather_z(pair, beside=(), after=None):
    quad = jnp.stack([pair, partner(pair, "core")])
    one = ahead(quad, 1)
    two = ahead(quad, 2)
    if beside:
        two, *beside = lax.optimization_barrier((two, *beside))
    three = ahead(two, 1)
    four = ahead(two[0], 2)
    if after:
        after = after(*beside)
        three, four, after = lax.optimization_barrier((three, four, after))
    mine = [one, two, three, four]
    theirs = [partner(block, "core") for block in mine]
    return (quad, mine, theirs), beside, after


def scatter_z(first, rest):
    next_two = jnp.concatenate([first(0, 2), rest(0, 2)]).astype(BF)
    s4 = first(2, 3)[0].astype(BF)
    hop = ahead(next_two, 1)
    four = ahead(s4, 2)
    three, one = hop[:2], hop[2:]
    s2 = rest(2, 4) + three.astype(F32)
    s2 = jnp.stack([s2[0] + four.astype(F32), s2[1]]).astype(BF)
    two = ahead(s2, 2)
    total = one.astype(F32) + two.astype(F32)
    across = partner(total[1].astype(BF), "core")
    return rest(4, 5)[0] + total[0] + across.astype(F32)


def scatter_dp(blocks):
    got = [lax.ppermute(blocks[k], "dp", shift_table(4, k)) for k in (2, 1, 3)]
    return [blocks[0]] + got


def summed(blocks):
    total = blocks[0].astype(F32)
    for block in blocks[1:]:
        total = total + block.astype(F32)
    return total


def gather_dp(block):
    got = {k: lax.ppermute(block, "dp", shift_table(4, 4 - k)) for k in (2, 1, 3)}
    return [block, got[1], got[2], got[3]]


def in_kernel(counts, squares, at, quad, *refs):
    mine, theirs, refs = refs[:4], refs[4:8], refs[8:]
    weights, refs = refs[: counts[0]], refs[counts[0] :]
    sides, refs = refs[: counts[1]], refs[counts[1] :]
    kvs, refs = refs[: counts[2]], refs[counts[2] :]
    outs, x, refs = refs[:4], refs[4], refs[5:]
    asides, refs = refs[: counts[1]], refs[counts[1] :]
    held, kv_rows, done = refs[:-2], refs[-2], refs[-1]
    copies = []
    for i, source in enumerate((*weights, *kvs, *sides)):
        copies.append(pltpu.make_async_copy(source, held[i], done.at[i]))
        copies[-1].start()
    weights, held = held[: counts[0]], held[counts[0] :]
    kvs, sides = held[: counts[2]], held[counts[2] :]
    waits = iter(copies)
    length, width = quad.shape[2], quad.shape[3]
    z0, core, xh, d = at[0], at[1], at[2], at[3]
    up = 2 * core - 1

    def place(block, z, feature_core):
        z = (z + 8) & 7
        first = pl.multiple_of((((z >> 1) - 2 * d) & 3) * length, length)
        for h in range(2):
            column = pl.multiple_of((((z & 1) * 2 + h) * 2 + feature_core) * width, width)
            x[pl.ds(first, length), pl.ds(column, width)] = block[h]

    for i in range(2):
        place(quad.at[i], z0, core ^ i)
    for hops in range(1, 4):
        for i in range(2):
            place(mine[hops - 1].at[i], z0 + up * hops, core ^ i)
            place(theirs[hops - 1].at[i], z0 - up * hops, core ^ i ^ 1)
    place(mine[3], z0 + 4, core)
    place(theirs[3], z0 + 4, core ^ 1)

    column = 0

    def put(product):
        for k in range(4):
            outs[k][:, column : column + product.shape[1]] = product[
                k * length : (k + 1) * length
            ].astype(BF)

    for weight in weights:
        next(waits).wait()
        put(jnp.dot(x[...], weight[...], preferred_element_type=F32))
        column += weight.shape[1]
    for kv in kvs:
        next(waits).wait()
        rows = kv.shape[2]
        for slot in range(4):
            member = ((slot & 1) ^ xh) * 2 + ((slot >> 1) ^ core)
            first = pl.multiple_of(member * rows, rows)
            for which in range(2):
                kv_rows[pl.ds(first + which * 4 * rows, rows), :] = kv[slot, which]
        put(
            lax.dot_general(
                x[...], kv_rows[...], (((1,), (1,)), ((), ())), preferred_element_type=F32
            )
        )
        column += 8 * rows
    if squares:
        for k in range(4):
            total = jnp.zeros((length, HD), F32)
            for lane in range(0, x.shape[1], HD):
                wide = x[k * length : (k + 1) * length, lane : lane + HD].astype(F32)
                total = total + wide * wide
            sums = jnp.sum(total, axis=1, keepdims=True)
            high = sums.astype(BF).astype(F32)
            lane = lax.broadcasted_iota(jnp.int32, (length, HD), 1)
            both = jnp.where(lane == 0, high, jnp.where(lane == 1, sums - high, 0.0))
            outs[k][:, column:] = both.astype(BF)
    for weight, aside in zip(sides, asides):
        next(waits).wait()
        product = jnp.dot(x[...], weight[...], preferred_element_type=F32).astype(BF)
        for k in range(4):
            first = pl.multiple_of(((k + d) & 3) * length, length)
            aside[pl.ds(first, length), :] = product[k * length : (k + 1) * length]


def gathered_dot(at, gathered, weights, kvs, squares, sides=()):
    quad, mine, theirs = gathered
    length, width = quad.shape[2:]
    depth = weights[0].shape[0]
    tokens = 4 * length
    columns = sum(w.shape[1] for w in weights) + sum(8 * kv.shape[2] for kv in kvs)
    wide = columns + (HD if squares else 0)
    kv_shape = (2 * HD, depth) if kvs else (16, HD)
    vmem = pl.BlockSpec(memory_space=pltpu.VMEM)
    blocks, heavy = [quad, *mine, *theirs], [*weights, *sides, *kvs]
    hbm = pl.BlockSpec(memory_space=pl.ANY)
    in_order = [*weights, *kvs, *sides]
    shapes = [(length, wide)] * 4 + [(tokens, depth)] + [(tokens, w.shape[1]) for w in sides]
    out = pl.pallas_call(
        functools.partial(in_kernel, (len(weights), len(sides), len(kvs)), squares),
        out_shape=tuple(jax.ShapeDtypeStruct(shape, BF) for shape in shapes),
        in_specs=[pl.BlockSpec(memory_space=pltpu.SMEM)]
        + [vmem] * len(blocks)
        + [hbm] * len(heavy),
        out_specs=(vmem,) * len(shapes),
        scratch_shapes=[pltpu.VMEM(w.shape, BF) for w in in_order]
        + [pltpu.VMEM(kv_shape, BF), pltpu.SemaphoreType.DMA((len(heavy),))],
        compiler_params=pltpu.CompilerParams(vmem_limit_bytes=32 << 20),
        cost_estimate=pl.CostEstimate(
            flops=2 * tokens * depth * columns,
            bytes_accessed=2 * depth * (columns + 2 * tokens),
            transcendentals=0,
        ),
    )(at, *blocks, *heavy)
    return out[:4], out[4], out[5:]


FIRST = ((3, 0), (3, 1), (4, 0))
REST = ((1, 0), (1, 1), (2, 0), (2, 1), (0, 0))


def out_kernel(count, at, *refs):
    contexts, weights = refs[:4], refs[4 : 4 + count]
    outs, rows = refs[4 + count : 8 + count], refs[8 + count]
    held, done = refs[9 + count : -1], refs[-1]
    copies = [pltpu.make_async_copy(weights[i], held[i], done.at[i]) for i in range(count)]
    for copy in copies:
        copy.start()
    weights = held
    length, width = outs[0].shape[3:]
    z0, own_core, d = at[0], at[1], at[3]
    for k in range(4):
        rows[k] = contexts[k][...]
    for copy in copies:
        copy.wait()
    for out, units, core in (
        (outs[0], FIRST, 1 - own_core),
        (outs[1], REST, 1 - own_core),
        (outs[2], FIRST, own_core),
        (outs[3], REST, own_core),
    ):
        for unit, (hops, other) in enumerate(units):
            z = (z0 + (1 - 2 * core) * hops + 8) & 7
            k = ((z >> 1) - 2 * d) & 3
            for h in range(2):
                column = (((z & 1) * 2 + h) * 2 + (core ^ other)) * width
                column = pl.multiple_of(column, width)
                terms = [
                    jnp.dot(
                        rows[k, i], weight[:, pl.ds(column, width)], preferred_element_type=F32
                    )
                    for i, weight in enumerate(weights)
                ]
                if count == 2:
                    terms[1] = terms[1] - terms[0]
                for i, term in enumerate(terms):
                    out[unit, i, h] = term.astype(out.dtype)


def out_blocks(at, contexts, weights):
    count, length, cols = contexts[0].shape
    depth = weights[0].shape[1]
    width = depth // 8
    vmem = pl.BlockSpec(memory_space=pltpu.VMEM)
    unit = (count, 2, length, width)
    return pl.pallas_call(
        functools.partial(out_kernel, count),
        out_shape=tuple(
            jax.ShapeDtypeStruct((len(units),) + unit, kind)
            for kind in (BF, F32)
            for units in (FIRST, REST)
        ),
        in_specs=[pl.BlockSpec(memory_space=pltpu.SMEM)]
        + [vmem] * 4
        + [pl.BlockSpec(memory_space=pl.ANY)] * count,
        out_specs=(vmem,) * 4,
        scratch_shapes=[pltpu.VMEM((4, count, length, cols), BF)]
        + [pltpu.VMEM(w.shape, BF) for w in weights]
        + [pltpu.SemaphoreType.DMA((count,))],
        compiler_params=pltpu.CompilerParams(vmem_limit_bytes=24 << 20),
        cost_estimate=pl.CostEstimate(
            flops=8 * count * length * cols * depth,
            bytes_accessed=count * (2 * cols * depth + 24 * length * depth),
            transcendentals=0,
        ),
    )(at, *contexts, *weights)


def attend(queries, keys, values, keep):
    length = queries.shape[0]
    four = queries.reshape(length, -1, HD)
    scores = jnp.einsum("igd,jd->gij", four, keys, preferred_element_type=F32) * HD ** (-0.5)
    probs = jax.nn.softmax(jnp.where(keep, scores, -1e30), axis=-1)
    probs_b = probs.astype(BF)
    context = jnp.einsum("gij,jd->igd", probs_b, values, preferred_element_type=F32)
    return context.astype(BF).reshape(length, -1), probs, probs_b, four


def local(
    tokens, par_gain, par_wq, par_wk, par_wv, par_wo, var_wq, var_wk, var_wv, var_wo, lin_w, windows
):
    section = lax.axis_index("section")
    d = lax.axis_index("dp")
    z = lax.axis_index(Z)
    xh = lax.axis_index("xh")
    core = lax.axis_index("core")
    _, length, width = tokens.shape
    rows = par_wq.shape[1]
    cols = par_wq.shape[2]
    kv_cols = par_wk.shape[2]
    n_dp = lax.axis_size("dp")
    all_tokens = n_dp * length
    inv_scale = float(all_tokens) ** (-0.5)
    n_model = par_gain.shape[1]
    gain = lax.dynamic_slice_in_dim(par_gain[0], d * rows, rows, 0)
    positions = jnp.arange(length, dtype=jnp.int32)
    causal = positions[None, :] <= positions[:, None]
    windowed = causal & (positions[None, :] > positions[:, None] - windows[0])
    at = jnp.stack([z, core, xh, d])

    tok = tokens[0]
    tok_pair = ordered(turned(tok), turned(tok, 1), xh)

    def gained(weight):
        return (weight[0].astype(F32) * gain[:, None]).astype(BF)

    def kv_weight(weight_k, weight_v):
        own = jnp.stack([gained(weight_k).T, gained(weight_v).T])
        two = jnp.stack([own, partner(own, "xh")])
        return jnp.concatenate([two, partner(two, "core")])

    par_q = gained(par_wq)
    par_kv = kv_weight(par_wk, par_wv)
    stu_q = gained(var_wq)
    stu_kv = kv_weight(var_wk, var_wv)
    lin_in = gained(lin_w)
    stu_back = var_wo[0].T

    def scale_of(summed):
        mean = (summed[:, 0:1] + summed[:, 1:2]) / n_model
        return lax.rsqrt(mean + 1e-05)

    def cut(sums, scale, first):
        heads = (sums[:, first : first + cols + 2 * HD] * scale).astype(BF)
        return heads[:, :cols], heads[:, cols : cols + HD], heads[:, cols + HD :]

    def summed_out(contexts, weights):
        contexts = gather_dp(contexts)
        first_away, rest_away, first, rest = out_blocks(at, contexts, weights)
        first_away = partner(first_away, "core")
        rest_away = partner(rest_away, "core")
        pair = scatter_z(
            lambda i, j: first[i:j] + first_away[i:j].astype(F32),
            lambda i, j: rest[i:j] + rest_away[i:j].astype(F32),
        )
        return pair.astype(BF), contexts

    ready = (par_q, par_kv, stu_q, stu_kv, lin_in, stu_back)
    got, ready, _ = gather_z(tok_pair, ready)
    par_q, par_kv, stu_q, stu_kv, lin_in, stu_back = ready
    part, _, _ = gathered_dot(at, got, [par_q], [par_kv], True)
    sums = summed(scatter_dp(part))
    scale = scale_of(sums[:, cols + 2 * HD :])
    context = attend(*cut(sums, scale, 0), causal)[0]
    pair, _ = summed_out(context[None], [par_wo[0]])
    pair = pair[0]
    to_next = [
        lax.ppermute(pair, ("section", "xh"), [(h, 2 + (h ^ flip)) for h in range(2)])
        for flip in range(2)
    ]
    next_pair = tok_pair.astype(F32) + (to_next[0].astype(F32) + to_next[1].astype(F32))
    in_pair = jnp.where(section == 0, tok_pair, next_pair.astype(BF))

    got, _, _ = gather_z(in_pair)
    part, x, (linear,) = gathered_dot(
        at, got, [par_q, stu_q], [par_kv, stu_kv], True, [lin_in]
    )
    sums = summed(scatter_dp(part))
    linear = lax.psum_scatter(linear, "dp", scatter_dimension=0, tiled=True)
    kv_first = 2 * cols
    scale = scale_of(sums[:, kv_first + 4 * HD :])
    heads = jnp.concatenate(
        [
            sums[:, :cols],
            sums[:, kv_first : kv_first + 2 * HD],
            sums[:, cols : 2 * cols],
            sums[:, kv_first + 2 * HD : kv_first + 4 * HD],
        ],
        axis=1,
    )
    par_context = attend(*cut(heads, scale, 0), causal)[0]
    queries, keys, values = cut(heads, scale, cols + 2 * HD)
    stu_context, probs, probs_b, query_four = attend(queries, keys, values, windowed)
    pair, contexts = summed_out(
        jnp.stack([par_context, stu_context]), [par_wo[0], var_wo[0]]
    )
    stu_all = jnp.concatenate([context[1] for context in contexts])
    pair = pair.astype(F32) + partner(pair, "xh").astype(F32)
    target, above = pair[0], pair[1]
    grad_student = (above * inv_scale).astype(BF)

    own_target = lax.dynamic_index_in_dim(target, xh, 0, keepdims=False)
    own_in = lax.dynamic_index_in_dim(in_pair, xh, 0, keepdims=False)
    own_out = (own_in.astype(F32) + own_target).astype(BF)
    back = turned_back(jnp.stack([own_out, own_target.astype(BF)]))

    def linear_grads(back):
        grad_linear = linear.astype(F32) * scale - back[1].astype(F32)
        grad_linear = (grad_linear * inv_scale).astype(BF)
        return gather_dp((grad_linear.astype(F32) * scale).astype(BF))

    got, (back,), grad_linear = gather_z(grad_student, (back,), linear_grads)
    layer_out = back[0]
    grad_linear = jnp.concatenate(grad_linear)

    part, gs, _ = gathered_dot(at, got, [stu_back], [], False)
    grad_context = summed(scatter_dp(part)).astype(BF)
    grad_four = grad_context.reshape(length, -1, HD)
    grad_probs = jnp.einsum("igd,jd->gij", grad_four, values, preferred_element_type=F32)
    grad_scores = probs * (grad_probs - jnp.sum(grad_probs * probs, axis=-1, keepdims=True))
    grad_scaled = (grad_scores * HD ** (-0.5)).astype(BF)
    grad_q = jnp.einsum("gij,jd->igd", grad_scaled, keys, preferred_element_type=F32)
    grad_q = (grad_q.reshape(length, cols) * scale).astype(BF)
    grad_k = jnp.einsum("gij,igd->dj", grad_scaled, query_four, preferred_element_type=F32)
    grad_v = jnp.einsum("gij,igd->dj", probs_b, grad_four, preferred_element_type=F32)
    members = HD // kv_cols
    parts = jnp.concatenate(
        [grad_k.reshape(members, kv_cols, length), grad_v.reshape(members, kv_cols, length)], axis=1
    )
    parts = (parts * scale.reshape(1, 1, length)).reshape(2, 2, 2 * kv_cols, length)

    def reduced(blocks, axis, at_axis, along):
        kept = lax.dynamic_index_in_dim(blocks, at_axis, along, keepdims=False)
        sent = lax.dynamic_index_in_dim(blocks, 1 - at_axis, along, keepdims=False)
        return kept + partner(sent.astype(BF), axis).astype(F32)

    parts = reduced(reduced(parts, "core", core, 1), "xh", xh, 0).astype(BF)
    grad_q = jnp.concatenate(gather_dp(grad_q))
    grad_q, parts = lax.optimization_barrier((grad_q, parts))
    grad_kv = jnp.concatenate(gather_dp(parts), axis=1)

    over_tokens = ((0,), (0,))
    column = gain[:, None]
    grad_wq = dot(x, grad_q, over_tokens) * column
    grad_wkv = dot(x, grad_kv, ((0,), (1,))) * column
    grad_wo = dot(stu_all, gs, over_tokens)
    grad_lin = dot(x, grad_linear, over_tokens) * column
    return (
        layer_out[None, None],
        grad_wq[None],
        grad_wkv[None, :, :kv_cols],
        grad_wkv[None, :, kv_cols:],
        grad_wo[None],
        grad_lin[None],
    )


def solution(mesh):
    sizes = (mesh.shape["section"], mesh.shape["dp"], 4, 2, 2, 2)
    fine = Mesh(mesh.devices.reshape(sizes), ("section", "dp") + MP)
    by_columns = P("section", "dp", MP)
    by_rows = P("section", MP, "dp")
    return jax.shard_map(
        local,
        mesh=fine,
        in_specs=(
            P("dp", None, MP),
            P("section", None),
            by_columns,
            by_columns,
            by_columns,
            by_rows,
            by_columns,
            by_columns,
            by_columns,
            by_rows,
            by_columns,
            P("section"),
        ),
        out_specs=(
            P("section", "dp", None, MP),
            by_columns,
            by_columns,
            by_columns,
            by_rows,
            by_columns,
        ),
        check_vma=False,
    )
```

```python
import functools

import jax
import jax.numpy as jnp
from jax import lax
from jax.experimental import pallas as pl
from jax.experimental.pallas import tpu as pltpu
from jax.sharding import Mesh, PartitionSpec as P

HQ = 64
KVH = 8
HD = 128
MP = ("zh", "zl", "xh", "core")
Z = ("zh", "zl")
BF = jnp.bfloat16
F32 = jnp.float32


def dot(left, right, dims):
    return lax.dot_general(left, right, (dims, ((), ())), preferred_element_type=F32)


def shift_table(count, distance):
    return [(i, (i + distance) % count) for i in range(count)]


def ordered(own, other, at):
    return jnp.where(at == 0, jnp.stack([own, other]), jnp.stack([other, own]))


def partner(block, axis):
    return lax.ppermute(block, axis, [(0, 1), (1, 0)])


def turn_table(flip):
    return [
        ((a * 4 + b) * 2 + h, (b * 4 + a) * 2 + (h ^ flip))
        for a in range(4)
        for b in range(4)
        for h in range(2)
    ]


def turned(block, flip=0):
    return lax.ppermute(block, ("dp", "zh", "xh"), turn_table(flip))


def ahead(block, hops):
    table = []
    for z in range(8):
        table.append((z * 2, (z + hops) % 8 * 2))
        table.append((z * 2 + 1, (z - hops) % 8 * 2 + 1))
    return lax.ppermute(block, Z + ("core",), table)


def gather_z(pair, beside=()):
    quad = jnp.stack([pair, partner(pair, "core")])
    one = ahead(quad, 1)
    two = ahead(quad, 2)
    if beside:
        two, *beside = lax.optimization_barrier((two, *beside))
    three = ahead(two, 1)
    four = ahead(two[0], 2)
    mine = [one, two, three, four]
    theirs = [partner(block, "core") for block in mine]
    return (quad, mine, theirs), beside


def scatter_z(first, rest):
    next_two = jnp.concatenate([first(0, 2), rest(0, 2)]).astype(BF)
    s4 = first(2, 3)[0].astype(BF)
    hop = ahead(next_two, 1)
    four = ahead(s4, 2)
    three, one = hop[:2], hop[2:]
    s2 = rest(2, 4) + three.astype(F32)
    s2 = jnp.stack([s2[0] + four.astype(F32), s2[1]]).astype(BF)
    two = ahead(s2, 2)
    total = one.astype(F32) + two.astype(F32)
    across = partner(total[1].astype(BF), "core")
    return rest(4, 5)[0] + total[0] + across.astype(F32)


def scatter_dp(blocks):
    got = [lax.ppermute(blocks[k], "dp", shift_table(4, k)) for k in (2, 1, 3)]
    return [blocks[0]] + got


def summed(blocks):
    total = blocks[0].astype(F32)
    for block in blocks[1:]:
        total = total + block.astype(F32)
    return total


def gather_dp(block):
    got = {k: lax.ppermute(block, "dp", shift_table(4, 4 - k)) for k in (2, 1, 3)}
    return [block, got[1], got[2], got[3]]


def in_kernel(counts, squares, at, quad, *refs):
    mine, theirs, refs = refs[:4], refs[4:8], refs[8:]
    weights, refs = refs[: counts[0]], refs[counts[0] :]
    sides, refs = refs[: counts[1]], refs[counts[1] :]
    kvs, refs = refs[: counts[2]], refs[counts[2] :]
    outs, x, asides, kv_rows = refs[:4], refs[4], refs[5:-1], refs[-1]
    length, width = quad.shape[2], quad.shape[3]
    z0, core, xh, d = at[0], at[1], at[2], at[3]
    up = 2 * core - 1

    def place(block, z, feature_core):
        z = (z + 8) & 7
        first = pl.multiple_of((((z >> 1) - d) & 3) * length, length)
        for h in range(2):
            column = pl.multiple_of((((z & 1) * 2 + h) * 2 + feature_core) * width, width)
            x[pl.ds(first, length), pl.ds(column, width)] = block[h]

    for i in range(2):
        place(quad.at[i], z0, core ^ i)
    for hops in range(1, 4):
        for i in range(2):
            place(mine[hops - 1].at[i], z0 + up * hops, core ^ i)
            place(theirs[hops - 1].at[i], z0 - up * hops, core ^ i ^ 1)
    place(mine[3], z0 + 4, core)
    place(theirs[3], z0 + 4, core ^ 1)

    column = 0

    def put(product):
        for k in range(4):
            outs[k][:, column : column + product.shape[1]] = product[
                k * length : (k + 1) * length
            ].astype(BF)

    for weight in weights:
        flat = weight.shape[1] == x.shape[1]
        dims = (((1,), (1 if flat else 0,)), ((), ()))
        put(lax.dot_general(x[...], weight[...], dims, preferred_element_type=F32))
        column += weight.shape[0 if flat else 1]
    for kv in kvs:
        rows = kv.shape[2]
        for slot in range(4):
            member = ((slot & 1) ^ xh) * 2 + ((slot >> 1) ^ core)
            first = pl.multiple_of(member * rows, rows)
            for which in range(2):
                kv_rows[pl.ds(first + which * 4 * rows, rows), :] = kv[slot, which]
        put(
            lax.dot_general(
                x[...], kv_rows[...], (((1,), (1,)), ((), ())), preferred_element_type=F32
            )
        )
        column += 8 * rows
    if squares:
        for k in range(4):
            total = jnp.zeros((length, HD), F32)
            for lane in range(0, x.shape[1], HD):
                wide = x[k * length : (k + 1) * length, lane : lane + HD].astype(F32)
                total = total + wide * wide
            sums = jnp.sum(total, axis=1, keepdims=True)
            high = sums.astype(BF).astype(F32)
            lane = lax.broadcasted_iota(jnp.int32, (length, HD), 1)
            both = jnp.where(lane == 0, high, jnp.where(lane == 1, sums - high, 0.0))
            outs[k][:, column:] = both.astype(BF)
    for weight, aside in zip(sides, asides):
        product = jnp.dot(x[...], weight[...], preferred_element_type=F32).astype(BF)
        for k in range(4):
            first = pl.multiple_of(((k + d) & 3) * length, length)
            aside[pl.ds(first, length), :] = product[k * length : (k + 1) * length]


def gathered_dot(at, gathered, weights, kvs, squares, sides=()):
    quad, mine, theirs = gathered
    length, width = quad.shape[2:]
    depth = 8 * width
    tokens = 4 * length
    columns = sum(w.size // depth for w in weights) + sum(8 * kv.shape[2] for kv in kvs)
    wide = columns + (HD if squares else 0)
    kv_shape = (2 * HD, depth) if kvs else (16, HD)
    vmem = pl.BlockSpec(memory_space=pltpu.VMEM)
    operands = [quad, *mine, *theirs, *weights, *sides, *kvs]
    shapes = [(length, wide)] * 4 + [(tokens, depth)] + [(tokens, w.shape[1]) for w in sides]
    out = pl.pallas_call(
        functools.partial(in_kernel, (len(weights), len(sides), len(kvs)), squares),
        out_shape=tuple(jax.ShapeDtypeStruct(shape, BF) for shape in shapes),
        in_specs=[pl.BlockSpec(memory_space=pltpu.SMEM)] + [vmem] * len(operands),
        out_specs=(vmem,) * len(shapes),
        scratch_shapes=[pltpu.VMEM(kv_shape, BF)],
        compiler_params=pltpu.CompilerParams(vmem_limit_bytes=32 << 20),
        cost_estimate=pl.CostEstimate(
            flops=2 * tokens * depth * columns,
            bytes_accessed=2 * depth * (columns + 2 * tokens),
            transcendentals=0,
        ),
    )(at, *operands)
    return out[:4], out[4], out[5:]


FIRST = ((3, 0), (3, 1), (4, 0))
REST = ((1, 0), (1, 1), (2, 0), (2, 1), (0, 0))


def out_kernel(count, at, *refs):
    contexts, weights = refs[:4], refs[4 : 4 + count]
    outs, rows = refs[4 + count : 8 + count], refs[8 + count]
    length, width = outs[0].shape[3:]
    z0, own_core, d = at[0], at[1], at[3]
    for k in range(4):
        rows[k] = contexts[k][...]
    for out, units, core in (
        (outs[0], FIRST, 1 - own_core),
        (outs[1], REST, 1 - own_core),
        (outs[2], FIRST, own_core),
        (outs[3], REST, own_core),
    ):
        for unit, (hops, other) in enumerate(units):
            z = (z0 + (1 - 2 * core) * hops + 8) & 7
            k = ((z >> 1) - d) & 3
            for h in range(2):
                column = (((z & 1) * 2 + h) * 2 + (core ^ other)) * width
                column = pl.multiple_of(column, width)
                terms = [
                    jnp.dot(
                        rows[k, i], weight[:, pl.ds(column, width)], preferred_element_type=F32
                    )
                    for i, weight in enumerate(weights)
                ]
                if count == 2:
                    terms[1] = terms[1] - terms[0]
                for i, term in enumerate(terms):
                    out[unit, i, h] = term.astype(out.dtype)


def out_blocks(at, contexts, weights):
    count, length, cols = contexts[0].shape
    depth = weights[0].shape[1]
    width = depth // 8
    vmem = pl.BlockSpec(memory_space=pltpu.VMEM)
    unit = (count, 2, length, width)
    return pl.pallas_call(
        functools.partial(out_kernel, count),
        out_shape=tuple(
            jax.ShapeDtypeStruct((len(units),) + unit, kind)
            for kind in (BF, F32)
            for units in (FIRST, REST)
        ),
        in_specs=[pl.BlockSpec(memory_space=pltpu.SMEM)] + [vmem] * (4 + count),
        out_specs=(vmem,) * 4,
        scratch_shapes=[pltpu.VMEM((4, count, length, cols), BF)],
        compiler_params=pltpu.CompilerParams(vmem_limit_bytes=24 << 20),
        cost_estimate=pl.CostEstimate(
            flops=8 * count * length * cols * depth,
            bytes_accessed=count * (2 * cols * depth + 24 * length * depth),
            transcendentals=0,
        ),
    )(at, *contexts, *weights)


def attend(queries, keys, values, keep):
    length = queries.shape[0]
    four = queries.reshape(length, -1, HD)
    scores = jnp.einsum("igd,jd->gij", four, keys, preferred_element_type=F32) * HD ** (-0.5)
    probs = jax.nn.softmax(jnp.where(keep, scores, -1e30), axis=-1)
    probs_b = probs.astype(BF)
    context = jnp.einsum("gij,jd->igd", probs_b, values, preferred_element_type=F32)
    return context.astype(BF).reshape(length, -1), probs, probs_b, four


def local(
    tokens, par_gain, par_wq, par_wk, par_wv, par_wo, var_wq, var_wk, var_wv, var_wo, lin_w, windows
):
    section = lax.axis_index("section")
    d = lax.axis_index("dp")
    z = lax.axis_index(Z)
    xh = lax.axis_index("xh")
    core = lax.axis_index("core")
    _, length, width = tokens.shape
    rows = par_wq.shape[1]
    cols = par_wq.shape[2]
    kv_cols = par_wk.shape[2]
    n_dp = lax.axis_size("dp")
    all_tokens = n_dp * length
    inv_scale = float(all_tokens) ** (-0.5)
    n_model = par_gain.shape[1]
    gain = lax.dynamic_slice_in_dim(par_gain[0], d * rows, rows, 0)
    positions = jnp.arange(length, dtype=jnp.int32)
    causal = positions[None, :] <= positions[:, None]
    windowed = causal & (positions[None, :] > positions[:, None] - windows[0])
    at = jnp.stack([z, core, xh, d])

    tok = tokens[0]
    tok_pair = ordered(turned(tok), turned(tok, 1), xh)

    def gained(weight):
        return (weight[0].astype(F32) * gain[:, None]).astype(BF)

    def kv_weight(weight_k, weight_v):
        own = jnp.stack([gained(weight_k).T, gained(weight_v).T])
        two = jnp.stack([own, partner(own, "xh")])
        return jnp.concatenate([two, partner(two, "core")])

    par_q = gained(par_wq)
    par_kv = kv_weight(par_wk, par_wv)
    stu_q = gained(var_wq)
    stu_kv = kv_weight(var_wk, var_wv)
    lin_in = gained(lin_w)

    def scale_of(summed):
        mean = (summed[:, 0:1] + summed[:, 1:2]) / n_model
        return lax.rsqrt(mean + 1e-05)

    def cut(sums, scale, first):
        heads = (sums[:, first : first + cols + 2 * HD] * scale).astype(BF)
        return heads[:, :cols], heads[:, cols : cols + HD], heads[:, cols + HD :]

    def summed_out(contexts, weights):
        contexts = gather_dp(contexts)
        first_away, rest_away, first, rest = out_blocks(at, contexts, weights)
        first_away = partner(first_away, "core")
        rest_away = partner(rest_away, "core")
        pair = scatter_z(
            lambda i, j: first[i:j] + first_away[i:j].astype(F32),
            lambda i, j: rest[i:j] + rest_away[i:j].astype(F32),
        )
        return pair.astype(BF), contexts

    got, (par_q, par_kv) = gather_z(tok_pair, (par_q, par_kv))
    part, _, _ = gathered_dot(at, got, [par_q], [par_kv], True)
    sums = summed(scatter_dp(part))
    scale = scale_of(sums[:, cols + 2 * HD :])
    context = attend(*cut(sums, scale, 0), causal)[0]
    context, stu_kv = lax.optimization_barrier((context, stu_kv))
    pair, _ = summed_out(context[None], [par_wo[0]])
    pair = pair[0]
    to_next = [
        lax.ppermute(pair, ("section", "xh"), [(h, 2 + (h ^ flip)) for h in range(2)])
        for flip in range(2)
    ]
    next_pair = tok_pair.astype(F32) + (to_next[0].astype(F32) + to_next[1].astype(F32))
    in_pair = jnp.where(section == 0, tok_pair, next_pair.astype(BF))

    got, (stu_q, lin_in) = gather_z(in_pair, (stu_q, lin_in))
    part, x, (linear,) = gathered_dot(
        at, got, [par_q, stu_q], [par_kv, stu_kv], True, [lin_in]
    )
    sums = summed(scatter_dp(part))
    linear = lax.psum_scatter(linear, "dp", scatter_dimension=0, tiled=True)
    kv_first = 2 * cols
    scale = scale_of(sums[:, kv_first + 4 * HD :])
    heads = jnp.concatenate(
        [
            sums[:, :cols],
            sums[:, kv_first : kv_first + 2 * HD],
            sums[:, cols : 2 * cols],
            sums[:, kv_first + 2 * HD : kv_first + 4 * HD],
        ],
        axis=1,
    )
    par_context = attend(*cut(heads, scale, 0), causal)[0]
    queries, keys, values = cut(heads, scale, cols + 2 * HD)
    stu_context, probs, probs_b, query_four = attend(queries, keys, values, windowed)
    pair, contexts = summed_out(
        jnp.stack([par_context, stu_context]), [par_wo[0], var_wo[0]]
    )
    stu_all = jnp.concatenate([context[1] for context in contexts])
    pair = pair.astype(F32) + partner(pair, "xh").astype(F32)
    target, above = pair[0], pair[1]
    grad_student = (above * inv_scale).astype(BF)

    own_target = lax.dynamic_index_in_dim(target, xh, 0, keepdims=False)
    own_in = lax.dynamic_index_in_dim(in_pair, xh, 0, keepdims=False)
    own_out = (own_in.astype(F32) + own_target).astype(BF)
    back = turned(jnp.stack([own_out, own_target.astype(BF)]))
    layer_out = back[0]
    got, (back_target,) = gather_z(grad_student, (back[1],))
    grad_linear = linear.astype(F32) * scale - back_target.astype(F32)
    grad_linear = (grad_linear * inv_scale).astype(BF)
    grad_linear = (grad_linear.astype(F32) * scale).astype(BF)

    part, gs, _ = gathered_dot(at, got, [var_wo[0]], [], False)
    grad_context = summed(scatter_dp(part)).astype(BF)
    grad_four = grad_context.reshape(length, -1, HD)
    grad_probs = jnp.einsum("igd,jd->gij", grad_four, values, preferred_element_type=F32)
    grad_scores = probs * (grad_probs - jnp.sum(grad_probs * probs, axis=-1, keepdims=True))
    grad_scaled = (grad_scores * HD ** (-0.5)).astype(BF)
    grad_q = jnp.einsum("gij,jd->igd", grad_scaled, keys, preferred_element_type=F32)
    grad_q = (grad_q.reshape(length, cols) * scale).astype(BF)
    grad_k = jnp.einsum("gij,igd->dj", grad_scaled, query_four, preferred_element_type=F32)
    grad_v = jnp.einsum("gij,igd->dj", probs_b, grad_four, preferred_element_type=F32)
    members = HD // kv_cols
    parts = jnp.concatenate(
        [grad_k.reshape(members, kv_cols, length), grad_v.reshape(members, kv_cols, length)], axis=1
    )
    parts = (parts * scale.reshape(1, 1, length)).reshape(2, 2, 2 * kv_cols, length)

    def reduced(blocks, axis, at_axis, along):
        kept = lax.dynamic_index_in_dim(blocks, at_axis, along, keepdims=False)
        sent = lax.dynamic_index_in_dim(blocks, 1 - at_axis, along, keepdims=False)
        return kept + partner(sent.astype(BF), axis).astype(F32)

    parts = reduced(reduced(parts, "core", core, 1), "xh", xh, 0).astype(BF)
    grads = jnp.concatenate(gather_dp(jnp.concatenate([grad_q, grad_linear], axis=1)))
    grad_q, grad_linear = grads[:, :cols], grads[:, cols:]
    grad_kv = jnp.concatenate(gather_dp(parts), axis=1)

    over_tokens = ((0,), (0,))
    column = gain[:, None]
    grad_wq = dot(x, grad_q, over_tokens) * column
    grad_wkv = dot(x, grad_kv, ((0,), (1,))) * column
    grad_wo = dot(stu_all, gs, over_tokens)
    grad_lin = dot(x, grad_linear, over_tokens) * column
    return (
        layer_out[None, None],
        grad_wq[None],
        grad_wkv[None, :, :kv_cols],
        grad_wkv[None, :, kv_cols:],
        grad_wo[None],
        grad_lin[None],
    )


def solution(mesh):
    sizes = (mesh.shape["section"], mesh.shape["dp"], 4, 2, 2, 2)
    fine = Mesh(mesh.devices.reshape(sizes), ("section", "dp") + MP)
    by_columns = P("section", "dp", MP)
    by_rows = P("section", MP, "dp")
    return jax.shard_map(
        local,
        mesh=fine,
        in_specs=(
            P("dp", None, MP),
            P("section", None),
            by_columns,
            by_columns,
            by_columns,
            by_rows,
            by_columns,
            by_columns,
            by_columns,
            by_rows,
            by_columns,
            P("section"),
        ),
        out_specs=(
            P("section", "dp", None, MP),
            by_columns,
            by_columns,
            by_columns,
            by_rows,
            by_columns,
        ),
        check_vma=False,
    )
```

```python
import functools

import jax
import jax.numpy as jnp
from jax import lax
from jax.experimental import pallas as pl
from jax.experimental.pallas import tpu as pltpu
from jax.sharding import Mesh, PartitionSpec as P

HQ = 64
KVH = 8
HD = 128
MP = ("zh", "zl", "xh", "core")
Z = ("zh", "zl")
BF = jnp.bfloat16
F32 = jnp.float32


def dot(left, right, dims):
    return lax.dot_general(left, right, (dims, ((), ())), preferred_element_type=F32)


def shift_table(count, distance):
    return [(i, (i + distance) % count) for i in range(count)]


def ordered(own, other, at):
    return jnp.where(at == 0, jnp.stack([own, other]), jnp.stack([other, own]))


def partner(block, axis):
    return lax.ppermute(block, axis, [(0, 1), (1, 0)])


def turn_table(flip):
    return [
        ((a * 4 + b) * 2 + h, (b * 4 + a) * 2 + (h ^ flip))
        for a in range(4)
        for b in range(4)
        for h in range(2)
    ]


def turned(block, flip=0):
    return lax.ppermute(block, ("dp", "zh", "xh"), turn_table(flip))


def ahead(block, hops):
    table = []
    for z in range(8):
        table.append((z * 2, (z + hops) % 8 * 2))
        table.append((z * 2 + 1, (z - hops) % 8 * 2 + 1))
    return lax.ppermute(block, Z + ("core",), table)


def gather_z(pair, beside=()):
    quad = jnp.stack([pair, partner(pair, "core")])
    one = ahead(quad, 1)
    two = ahead(quad, 2)
    if beside:
        two, *beside = lax.optimization_barrier((two, *beside))
    three = ahead(two, 1)
    four = ahead(two[0], 2)
    mine = [one, two, three, four]
    theirs = [partner(block, "core") for block in mine]
    return (quad, mine, theirs), beside


def scatter_z(first, rest, by_one):
    if by_one:
        moved = ahead(first(2, 3)[0].astype(BF), 1).astype(F32)
        moved = jnp.stack([first(0, 1)[0] + moved, first(1, 2)[0]]).astype(BF)
        moved = (rest(2, 4) + ahead(moved, 1).astype(F32)).astype(BF)
        moved = (rest(0, 2) + ahead(moved, 1).astype(F32)).astype(BF)
        total = ahead(moved, 1).astype(F32)
    else:
        s3, s4 = first(0, 2).astype(BF), first(2, 3)[0].astype(BF)
        s1 = rest(0, 2).astype(BF)
        three = ahead(s3, 1)
        four = ahead(s4, 2)
        one = ahead(s1, 1)
        s2 = rest(2, 4) + three.astype(F32)
        s2 = jnp.stack([s2[0] + four.astype(F32), s2[1]]).astype(BF)
        two = ahead(s2, 2)
        total = one.astype(F32) + two.astype(F32)
    across = partner(total[1].astype(BF), "core")
    return rest(4, 5)[0] + total[0] + across.astype(F32)


def scatter_dp(blocks):
    got = [lax.ppermute(blocks[k], "dp", shift_table(4, k)) for k in (2, 1, 3)]
    return [blocks[0]] + got


def summed(blocks):
    total = blocks[0].astype(F32)
    for block in blocks[1:]:
        total = total + block.astype(F32)
    return total


def gather_dp(block):
    got = {k: lax.ppermute(block, "dp", shift_table(4, 4 - k)) for k in (2, 1, 3)}
    return [block, got[1], got[2], got[3]]


def in_kernel(counts, squares, at, quad, *refs):
    mine, theirs, refs = refs[:4], refs[4:8], refs[8:]
    weights, refs = refs[: counts[0]], refs[counts[0] :]
    sides, refs = refs[: counts[1]], refs[counts[1] :]
    kvs, refs = refs[: counts[2]], refs[counts[2] :]
    outs, x, asides, kv_rows = refs[:4], refs[4], refs[5:-1], refs[-1]
    length, width = quad.shape[2], quad.shape[3]
    z0, core, xh, d = at[0], at[1], at[2], at[3]
    up = 2 * core - 1

    def place(block, z, feature_core):
        z = (z + 8) & 7
        first = pl.multiple_of((((z >> 1) - d) & 3) * length, length)
        for h in range(2):
            column = pl.multiple_of((((z & 1) * 2 + h) * 2 + feature_core) * width, width)
            x[pl.ds(first, length), pl.ds(column, width)] = block[h]

    for i in range(2):
        place(quad.at[i], z0, core ^ i)
    for hops in range(1, 4):
        for i in range(2):
            place(mine[hops - 1].at[i], z0 + up * hops, core ^ i)
            place(theirs[hops - 1].at[i], z0 - up * hops, core ^ i ^ 1)
    place(mine[3], z0 + 4, core)
    place(theirs[3], z0 + 4, core ^ 1)

    column = 0

    def put(product):
        for k in range(4):
            outs[k][:, column : column + product.shape[1]] = product[
                k * length : (k + 1) * length
            ].astype(BF)

    for weight in weights:
        flat = weight.shape[1] == x.shape[1]
        dims = (((1,), (1 if flat else 0,)), ((), ()))
        put(lax.dot_general(x[...], weight[...], dims, preferred_element_type=F32))
        column += weight.shape[0 if flat else 1]
    for kv in kvs:
        rows = kv.shape[2]
        for slot in range(4):
            member = ((slot & 1) ^ xh) * 2 + ((slot >> 1) ^ core)
            first = pl.multiple_of(member * rows, rows)
            for which in range(2):
                kv_rows[pl.ds(first + which * 4 * rows, rows), :] = kv[slot, which]
        put(
            lax.dot_general(
                x[...], kv_rows[...], (((1,), (1,)), ((), ())), preferred_element_type=F32
            )
        )
        column += 8 * rows
    if squares:
        for k in range(4):
            total = jnp.zeros((length, HD), F32)
            for lane in range(0, x.shape[1], HD):
                wide = x[k * length : (k + 1) * length, lane : lane + HD].astype(F32)
                total = total + wide * wide
            sums = jnp.sum(total, axis=1, keepdims=True)
            high = sums.astype(BF).astype(F32)
            lane = lax.broadcasted_iota(jnp.int32, (length, HD), 1)
            both = jnp.where(lane == 0, high, jnp.where(lane == 1, sums - high, 0.0))
            outs[k][:, column:] = both.astype(BF)
    for weight, aside in zip(sides, asides):
        product = jnp.dot(x[...], weight[...], preferred_element_type=F32).astype(BF)
        for k in range(4):
            first = pl.multiple_of(((k + d) & 3) * length, length)
            aside[pl.ds(first, length), :] = product[k * length : (k + 1) * length]


def gathered_dot(at, gathered, weights, kvs, squares, sides=()):
    quad, mine, theirs = gathered
    length, width = quad.shape[2:]
    depth = 8 * width
    tokens = 4 * length
    columns = sum(w.size // depth for w in weights) + sum(8 * kv.shape[2] for kv in kvs)
    wide = columns + (HD if squares else 0)
    kv_shape = (2 * HD, depth) if kvs else (16, HD)
    vmem = pl.BlockSpec(memory_space=pltpu.VMEM)
    operands = [quad, *mine, *theirs, *weights, *sides, *kvs]
    shapes = [(length, wide)] * 4 + [(tokens, depth)] + [(tokens, w.shape[1]) for w in sides]
    out = pl.pallas_call(
        functools.partial(in_kernel, (len(weights), len(sides), len(kvs)), squares),
        out_shape=tuple(jax.ShapeDtypeStruct(shape, BF) for shape in shapes),
        in_specs=[pl.BlockSpec(memory_space=pltpu.SMEM)] + [vmem] * len(operands),
        out_specs=(vmem,) * len(shapes),
        scratch_shapes=[pltpu.VMEM(kv_shape, BF)],
        compiler_params=pltpu.CompilerParams(vmem_limit_bytes=32 << 20),
        cost_estimate=pl.CostEstimate(
            flops=2 * tokens * depth * columns,
            bytes_accessed=2 * depth * (columns + 2 * tokens),
            transcendentals=0,
        ),
    )(at, *operands)
    return out[:4], out[4], out[5:]


FIRST = ((3, 0), (3, 1), (4, 0))
REST = ((1, 0), (1, 1), (2, 0), (2, 1), (0, 0))


def out_kernel(count, at, *refs):
    contexts, weights = refs[:4], refs[4 : 4 + count]
    outs, rows = refs[4 + count : 8 + count], refs[8 + count]
    length, width = outs[0].shape[3:]
    z0, own_core, d = at[0], at[1], at[3]
    for k in range(4):
        rows[k] = contexts[k][...]
    for out, units, core in (
        (outs[0], FIRST, 1 - own_core),
        (outs[1], REST, 1 - own_core),
        (outs[2], FIRST, own_core),
        (outs[3], REST, own_core),
    ):
        for unit, (hops, other) in enumerate(units):
            z = (z0 + (1 - 2 * core) * hops + 8) & 7
            k = ((z >> 1) - d) & 3
            for h in range(2):
                column = (((z & 1) * 2 + h) * 2 + (core ^ other)) * width
                column = pl.multiple_of(column, width)
                terms = [
                    jnp.dot(
                        rows[k, i], weight[:, pl.ds(column, width)], preferred_element_type=F32
                    )
                    for i, weight in enumerate(weights)
                ]
                if count == 2:
                    terms[1] = terms[1] - terms[0]
                for i, term in enumerate(terms):
                    out[unit, i, h] = term.astype(out.dtype)


def out_blocks(at, contexts, weights):
    count, length, cols = contexts[0].shape
    depth = weights[0].shape[1]
    width = depth // 8
    vmem = pl.BlockSpec(memory_space=pltpu.VMEM)
    unit = (count, 2, length, width)
    return pl.pallas_call(
        functools.partial(out_kernel, count),
        out_shape=tuple(
            jax.ShapeDtypeStruct((len(units),) + unit, kind)
            for kind in (BF, F32)
            for units in (FIRST, REST)
        ),
        in_specs=[pl.BlockSpec(memory_space=pltpu.SMEM)] + [vmem] * (4 + count),
        out_specs=(vmem,) * 4,
        scratch_shapes=[pltpu.VMEM((4, count, length, cols), BF)],
        compiler_params=pltpu.CompilerParams(vmem_limit_bytes=24 << 20),
        cost_estimate=pl.CostEstimate(
            flops=8 * count * length * cols * depth,
            bytes_accessed=count * (2 * cols * depth + 24 * length * depth),
            transcendentals=0,
        ),
    )(at, *contexts, *weights)


def attend(queries, keys, values, keep):
    length = queries.shape[0]
    four = queries.reshape(length, -1, HD)
    scores = jnp.einsum("igd,jd->gij", four, keys, preferred_element_type=F32) * HD ** (-0.5)
    probs = jax.nn.softmax(jnp.where(keep, scores, -1e30), axis=-1)
    probs_b = probs.astype(BF)
    context = jnp.einsum("gij,jd->igd", probs_b, values, preferred_element_type=F32)
    return context.astype(BF).reshape(length, -1), probs, probs_b, four


def local(
    tokens, par_gain, par_wq, par_wk, par_wv, par_wo, var_wq, var_wk, var_wv, var_wo, lin_w, windows
):
    section = lax.axis_index("section")
    d = lax.axis_index("dp")
    z = lax.axis_index(Z)
    xh = lax.axis_index("xh")
    core = lax.axis_index("core")
    _, length, width = tokens.shape
    rows = par_wq.shape[1]
    cols = par_wq.shape[2]
    kv_cols = par_wk.shape[2]
    n_dp = lax.axis_size("dp")
    all_tokens = n_dp * length
    inv_scale = float(all_tokens) ** (-0.5)
    n_model = par_gain.shape[1]
    gain = lax.dynamic_slice_in_dim(par_gain[0], d * rows, rows, 0)
    positions = jnp.arange(length, dtype=jnp.int32)
    causal = positions[None, :] <= positions[:, None]
    windowed = causal & (positions[None, :] > positions[:, None] - windows[0])
    at = jnp.stack([z, core, xh, d])

    tok = tokens[0]
    tok_pair = ordered(turned(tok), turned(tok, 1), xh)

    def gained(weight):
        return (weight[0].astype(F32) * gain[:, None]).astype(BF)

    def kv_weight(weight_k, weight_v):
        own = jnp.stack([gained(weight_k).T, gained(weight_v).T])
        two = jnp.stack([own, partner(own, "xh")])
        return jnp.concatenate([two, partner(two, "core")])

    par_q = gained(par_wq)
    par_kv = kv_weight(par_wk, par_wv)
    stu_q = gained(var_wq)
    stu_kv = kv_weight(var_wk, var_wv)
    lin_in = gained(lin_w)

    def scale_of(summed):
        mean = (summed[:, 0:1] + summed[:, 1:2]) / n_model
        return lax.rsqrt(mean + 1e-05)

    def cut(sums, scale, first):
        heads = (sums[:, first : first + cols + 2 * HD] * scale).astype(BF)
        return heads[:, :cols], heads[:, cols : cols + HD], heads[:, cols + HD :]

    def summed_out(contexts, weights):
        contexts = gather_dp(contexts)
        first_away, rest_away, first, rest = out_blocks(at, contexts, weights)
        first_away = partner(first_away, "core")
        rest_away = partner(rest_away, "core")
        pair = scatter_z(
            lambda i, j: first[i:j] + first_away[i:j].astype(F32),
            lambda i, j: rest[i:j] + rest_away[i:j].astype(F32),
            len(weights) > 1,
        )
        return pair.astype(BF), contexts

    got, (par_q, par_kv) = gather_z(tok_pair, (par_q, par_kv))
    part, _, _ = gathered_dot(at, got, [par_q], [par_kv], True)
    sums = summed(scatter_dp(part))
    scale = scale_of(sums[:, cols + 2 * HD :])
    context = attend(*cut(sums, scale, 0), causal)[0]
    pair, _ = summed_out(context[None], [par_wo[0]])
    pair = pair[0]
    to_next = [
        lax.ppermute(pair, ("section", "xh"), [(h, 2 + (h ^ flip)) for h in range(2)])
        for flip in range(2)
    ]
    next_pair = tok_pair.astype(F32) + (to_next[0].astype(F32) + to_next[1].astype(F32))
    in_pair = jnp.where(section == 0, tok_pair, next_pair.astype(BF))

    got, (stu_q, stu_kv, lin_in) = gather_z(in_pair, (stu_q, stu_kv, lin_in))
    part, x, (linear,) = gathered_dot(
        at, got, [par_q, stu_q], [par_kv, stu_kv], True, [lin_in]
    )
    sums = summed(scatter_dp(part))
    linear = lax.psum_scatter(linear, "dp", scatter_dimension=0, tiled=True)
    kv_first = 2 * cols
    scale = scale_of(sums[:, kv_first + 4 * HD :])
    heads = jnp.concatenate(
        [
            sums[:, :cols],
            sums[:, kv_first : kv_first + 2 * HD],
            sums[:, cols : 2 * cols],
            sums[:, kv_first + 2 * HD : kv_first + 4 * HD],
        ],
        axis=1,
    )
    par_context = attend(*cut(heads, scale, 0), causal)[0]
    queries, keys, values = cut(heads, scale, cols + 2 * HD)
    stu_context, probs, probs_b, query_four = attend(queries, keys, values, windowed)
    pair, contexts = summed_out(
        jnp.stack([par_context, stu_context]), [par_wo[0], var_wo[0]]
    )
    stu_all = jnp.concatenate([context[1] for context in contexts])
    pair = pair.astype(F32) + partner(pair, "xh").astype(F32)
    target, above = pair[0], pair[1]
    grad_student = (above * inv_scale).astype(BF)

    own_target = lax.dynamic_index_in_dim(target, xh, 0, keepdims=False)
    own_in = lax.dynamic_index_in_dim(in_pair, xh, 0, keepdims=False)
    own_out = (own_in.astype(F32) + own_target).astype(BF)
    back = turned(jnp.stack([own_out, own_target.astype(BF)]))
    layer_out = back[0]
    got, (back_target,) = gather_z(grad_student, (back[1],))
    grad_linear = linear.astype(F32) * scale - back_target.astype(F32)
    grad_linear = (grad_linear * inv_scale).astype(BF)
    grad_linear = (grad_linear.astype(F32) * scale).astype(BF)

    part, gs, _ = gathered_dot(at, got, [var_wo[0]], [], False)
    grad_context = summed(scatter_dp(part)).astype(BF)
    grad_four = grad_context.reshape(length, -1, HD)
    grad_probs = jnp.einsum("igd,jd->gij", grad_four, values, preferred_element_type=F32)
    grad_scores = probs * (grad_probs - jnp.sum(grad_probs * probs, axis=-1, keepdims=True))
    grad_scaled = (grad_scores * HD ** (-0.5)).astype(BF)
    grad_q = jnp.einsum("gij,jd->igd", grad_scaled, keys, preferred_element_type=F32)
    grad_q = (grad_q.reshape(length, cols) * scale).astype(BF)
    grad_k = jnp.einsum("gij,igd->dj", grad_scaled, query_four, preferred_element_type=F32)
    grad_v = jnp.einsum("gij,igd->dj", probs_b, grad_four, preferred_element_type=F32)
    members = HD // kv_cols
    parts = jnp.concatenate(
        [grad_k.reshape(members, kv_cols, length), grad_v.reshape(members, kv_cols, length)], axis=1
    )
    parts = (parts * scale.reshape(1, 1, length)).reshape(2, 2, 2 * kv_cols, length)

    def reduced(blocks, axis, at_axis, along):
        kept = lax.dynamic_index_in_dim(blocks, at_axis, along, keepdims=False)
        sent = lax.dynamic_index_in_dim(blocks, 1 - at_axis, along, keepdims=False)
        return kept + partner(sent.astype(BF), axis).astype(F32)

    parts = reduced(reduced(parts, "core", core, 1), "xh", xh, 0).astype(BF)
    grads = jnp.concatenate(gather_dp(jnp.concatenate([grad_q, grad_linear], axis=1)))
    grad_q, grad_linear = grads[:, :cols], grads[:, cols:]
    grad_kv = jnp.concatenate(gather_dp(parts), axis=1)

    over_tokens = ((0,), (0,))
    column = gain[:, None]
    grad_wq = dot(x, grad_q, over_tokens) * column
    grad_wkv = dot(x, grad_kv, ((0,), (1,))) * column
    grad_wo = dot(stu_all, gs, over_tokens)
    grad_lin = dot(x, grad_linear, over_tokens) * column
    return (
        layer_out[None, None],
        grad_wq[None],
        grad_wkv[None, :, :kv_cols],
        grad_wkv[None, :, kv_cols:],
        grad_wo[None],
        grad_lin[None],
    )


def solution(mesh):
    sizes = (mesh.shape["section"], mesh.shape["dp"], 4, 2, 2, 2)
    fine = Mesh(mesh.devices.reshape(sizes), ("section", "dp") + MP)
    by_columns = P("section", "dp", MP)
    by_rows = P("section", MP, "dp")
    return jax.shard_map(
        local,
        mesh=fine,
        in_specs=(
            P("dp", None, MP),
            P("section", None),
            by_columns,
            by_columns,
            by_columns,
            by_rows,
            by_columns,
            by_columns,
            by_columns,
            by_rows,
            by_columns,
            P("section"),
        ),
        out_specs=(
            P("section", "dp", None, MP),
            by_columns,
            by_columns,
            by_columns,
            by_rows,
            by_columns,
        ),
        check_vma=False,
    )
```
